128 devices in a mesh: row: 8 (over z, x_hi), col: 16 (over y, x_lo, core).
Axes of the slice: x: 4 (x_hi: 2, x_lo: 2; x = x_hi * 2 + x_lo), y: 4, z: 4, core: 2. Of those that a mesh axis runs over, the one named last changes fastest.
Arguments:
- tokens: bfloat16 [1024, 8192], P('row', 'col'), may hold values from -6 to 6
- out_grad: bfloat16 [1024, 8192], P('row', 'col'), may hold values from -6 to 6
- gate_weight: bfloat16 [8192, 14336], P('col', 'row'), may hold values from -0.0625 to 0.0625
- up_weight: bfloat16 [8192, 14336], P('col', 'row'), may hold values from -0.0625 to 0.0625
- down_weight: bfloat16 [14336, 8192], P('row', 'col'), may hold values from -0.046875 to 0.046875
Outputs:
- tokens_grad: bfloat16 [1024, 8192], P('row', 'col')
- gate_grad: bfloat16 [8192, 14336], P('col', 'row')
- up_grad: bfloat16 [8192, 14336], P('col', 'row')
- down_grad: bfloat16 [14336, 8192], P('row', 'col')
The draws below stay inside these ranges and needn't reach their ends.
All inputs are finite; a program needn't handle non-finite values.
Results may differ from the reference program's by a relative error of at most 0.005.
Values may be sent and summed in bfloat16 or wider, within the bound.
No kernel may reach another device: no remote copies, remote signals or barrier semaphores. Data moves between devices by JAX's collectives and lax.ppermute only.
A program may use at most 192 MiB of HBM per device.

```python
import jax
import jax.numpy as jnp
from jax import lax

D = 8192
FF = 14336
TOKENS = 1024


def level_of(stream_key, extent, shards, smallest, high):
    level, own = 1.0, jax.random.fold_in(stream_key, 6)
    for axis_at, parts in shards:
        draws = jnp.exp(jax.random.uniform(jax.random.fold_in(own, axis_at), (parts,), jnp.float32, smallest / len(shards), high / len(shards)))
        level = level * jnp.repeat(draws, extent[axis_at] // parts).reshape([-1 if axis == axis_at else 1 for axis in range(len(extent))])
    return level


def noise(key, shape, deviation, bound, pieces=(), held_as=jnp.bfloat16):
    drawn = deviation * jax.random.normal(key, shape, jnp.float32)
    if pieces:
        drawn = drawn * level_of(key, shape, pieces, -0.22, 0.18)
    return jnp.clip(drawn, -bound, bound).astype(held_as)


def setup_inputs(seed: int = 0) -> dict:
    seeds = jax.random.split(jax.random.key(seed), 6)
    tokens = noise(seeds[0], (TOKENS, D), 1.0, 6.0, ((0, 8), (1, 16)))
    out_grad = noise(seeds[1], (TOKENS, D), 1.0, 6.0, ((0, 8), (1, 16)))
    gate_weight = noise(seeds[2], (D, FF), D ** -0.5, 0.0625, ((0, 16), (1, 8)))
    up_weight = noise(seeds[3], (D, FF), D ** -0.5, 0.0625, ((0, 16), (1, 8)))
    down_weight = noise(seeds[4], (FF, D), FF ** -0.5, 0.046875, ((0, 8), (1, 16)))
    return dict(tokens=tokens, out_grad=out_grad, gate_weight=gate_weight, up_weight=up_weight, down_weight=down_weight)


def reference(tokens, out_grad, gate_weight, up_weight, down_weight):
    gate = jnp.dot(tokens, gate_weight, preferred_element_type=jnp.float32)
    upper = jnp.dot(tokens, up_weight, preferred_element_type=jnp.float32)
    hidden_grad = lax.dot_general(out_grad, down_weight, (((1,), (1,)), ((), ())), preferred_element_type=jnp.float32)
    sig = jax.nn.sigmoid(gate)
    silu_val = gate * sig
    hidden = (silu_val * upper).astype(jnp.bfloat16)
    up_part = (hidden_grad * silu_val).astype(jnp.bfloat16)
    gate_part = (hidden_grad * upper * sig * (1.0 + gate * (1.0 - sig))).astype(jnp.bfloat16)
    down_grad = jnp.dot(hidden.T, out_grad, preferred_element_type=jnp.float32).astype(jnp.bfloat16)
    gate_grad = jnp.dot(tokens.T, gate_part, preferred_element_type=jnp.float32).astype(jnp.bfloat16)
    up_grad = jnp.dot(tokens.T, up_part, preferred_element_type=jnp.float32).astype(jnp.bfloat16)
    tokens_grad = jnp.dot(gate_part, gate_weight.T, preferred_element_type=jnp.float32)
    tokens_grad = tokens_grad + jnp.dot(up_part, up_weight.T, preferred_element_type=jnp.float32)
    return tokens_grad.astype(jnp.bfloat16), gate_grad, up_grad, down_grad
```

```python
import jax
import jax.numpy as jnp
from jax import lax
from jax.experimental import pallas as pl
from jax.experimental.pallas import tpu as pltpu
from jax.sharding import Mesh
from jax.sharding import PartitionSpec as P

AXES = {"z": 4, "xh": 2, "y": 4, "xl": 2, "core": 2}
LANE = 128
contract_first = (((0,), (0,)), ((), ()))
contract_last = (((1,), (1,)), ((), ()))
f32 = jnp.float32
bf16 = jnp.bfloat16


def move(a, axis, by):
    n = AXES[axis]
    return lax.ppermute(a, axis, [(i, (i + by) % n) for i in range(n)])


def move2(a, dz, dx):
    pairs = [(z * 2 + x, ((z + dz) % 4) * 2 + (x + dx) % 2) for z in range(4) for x in range(2)]
    return lax.ppermute(a, ("z", "xh"), pairs)


def dot(a, b, dims):
    return lax.dot_general(a, b, dims, preferred_element_type=f32)


plain = (((1,), (0,)), ((), ()))


def forward_kernel(own, oth, gu_own, gu_oth, d_own, d_oth, keep, second, plus, minus):
    half = own.shape[1] // 2
    gu = dot(own[:, :half], gu_own[...], plain) + dot(oth[:, :half], gu_oth[...], plain)
    hg = dot(own[:, half:], d_own[...], contract_last) + dot(oth[:, half:], d_oth[...], contract_last)
    for part, cols in ((gu, slice(0, 2 * LANE)), (hg, slice(2 * LANE, 3 * LANE))):
        keep[:, cols] = part[0:64]
        second[0:32, cols] = part[64:96]
        second[32:64, cols] = part[224:256]
        plus[:, cols] = part[96:160].astype(bf16)
        minus[:, cols] = part[160:224].astype(bf16)


def forward(own, oth, gu_own, gu_oth, d_own, d_oth):
    rows, both = own.shape
    depth = both // 2
    tiles = d_own.shape[0] // LANE
    wide = 3 * LANE * tiles
    whole = pl.BlockSpec((rows, both), lambda t: (0, 0))
    gu = pl.BlockSpec((depth, 2 * LANE), lambda t: (0, t))
    d = pl.BlockSpec((LANE, depth), lambda t: (t, 0))
    out = pl.BlockSpec((64, 3 * LANE), lambda t: (0, t))
    return pl.pallas_call(
        forward_kernel,
        grid=(tiles,),
        in_specs=[whole, whole, gu, gu, d, d],
        out_specs=[out] * 4,
        out_shape=[
            jax.ShapeDtypeStruct((64, wide), f32),
            jax.ShapeDtypeStruct((64, wide), f32),
            jax.ShapeDtypeStruct((64, wide), bf16),
            jax.ShapeDtypeStruct((64, wide), bf16),
        ],
        cost_estimate=pl.CostEstimate(
            flops=2 * rows * 2 * depth * wide, bytes_accessed=4 * depth * wide, transcendentals=0
        ),
        compiler_params=pltpu.CompilerParams(vmem_limit_bytes=24 << 20),
        name="forward",
    )(own, oth, gu_own, gu_oth, d_own, d_oth)


def activate_kernel(keep, minus, second, across, out):
    tiles = out.shape[1] // (3 * LANE)
    for t in range(tiles):
        def total(j):
            cols = slice((3 * t + j) * LANE, (3 * t + j + 1) * LANE)
            return (
                keep[0:32, cols]
                + minus[32:64, cols].astype(f32)
                + second[:, cols].astype(f32)
                + across[:, cols]
            )

        gate, upper, hidden_grad = total(0), total(1), total(2)
        sig = jax.nn.sigmoid(gate)
        silu = gate * sig
        base = 3 * t * LANE
        out[:, base : base + LANE] = (silu * upper).astype(bf16)
        out[:, base + LANE : base + 2 * LANE] = (
            hidden_grad * upper * sig * (1.0 + gate * (1.0 - sig))
        ).astype(bf16)
        out[:, base + 2 * LANE : base + 3 * LANE] = (hidden_grad * silu).astype(bf16)


def activate(keep, minus, second, across):
    return pl.pallas_call(
        activate_kernel,
        out_shape=jax.ShapeDtypeStruct(second.shape, bf16),
        cost_estimate=pl.CostEstimate(flops=2000000, bytes_accessed=1500000, transcendentals=30000),
        compiler_params=pltpu.CompilerParams(vmem_limit_bytes=8 << 20),
        name="activate",
    )(keep, minus, second, across)


def ordered(core, mine, other, j):
    cols = slice(j * LANE, (j + 1) * LANE)
    a, b = mine[:, cols], other[:, cols]
    first = core == 0
    return jnp.concatenate([jnp.where(first, a, b), jnp.where(first, b, a)], axis=1)


def back_kernel(core, mine, other, wg, wu, near, far, total):
    t = pl.program_id(0)

    @pl.when(t == 0)
    def _():
        total[...] = jnp.zeros_like(total)

    c = core[0]
    total[...] += dot(ordered(c, mine, other, 1), wg[...], contract_last) + dot(
        ordered(c, mine, other, 2), wu[...], contract_last
    )

    @pl.when(t == pl.num_programs(0) - 1)
    def _():
        for b in range(8):
            near[16 * b : 16 * b + 16, :] = total[32 * b : 32 * b + 16, :].astype(near.dtype)
            far[16 * b : 16 * b + 16, :] = total[32 * b + 16 : 32 * b + 32, :].astype(far.dtype)


def back(core, mine, other, wg, wu, near_type):
    rows, wide = mine.shape
    depth = wg.shape[0]
    tiles = wide // (3 * LANE)
    act = pl.BlockSpec((rows, 3 * LANE), lambda t: (0, t))
    weight = pl.BlockSpec((depth, 2 * LANE), lambda t: (0, t))
    out = pl.BlockSpec((rows // 2, depth), lambda t: (0, 0))
    return pl.pallas_call(
        back_kernel,
        grid=(tiles,),
        in_specs=[pl.BlockSpec(memory_space=pltpu.SMEM), act, act, weight, weight],
        out_specs=[out, out],
        out_shape=[
            jax.ShapeDtypeStruct((rows // 2, depth), near_type),
            jax.ShapeDtypeStruct((rows // 2, depth), bf16),
        ],
        scratch_shapes=[pltpu.VMEM((rows, depth), f32)],
        cost_estimate=pl.CostEstimate(
            flops=8 * rows * depth * tiles * 2 * LANE, bytes_accessed=8 * depth * tiles * LANE, transcendentals=0
        ),
        compiler_params=pltpu.CompilerParams(vmem_limit_bytes=24 << 20),
        name="back",
    )(core, mine, other, wg, wu)


def weights_kernel(core, *refs):
    mine, other, turned, direct = refs[0:4], refs[4:8], refs[8:12], refs[12:16]
    gate_out, up_out, down_out = refs[16:]
    c = core[0]
    half = direct[0].shape[1] // 2
    both = down = None
    for m, o, xt, xg in zip(mine, other, turned, direct):
        pair = jnp.concatenate([ordered(c, m, o, 1), ordered(c, m, o, 2)], axis=1)
        first = dot(xt[:half, :], pair, plain)
        second = dot(ordered(c, m, o, 0), xg[:, half:], contract_first)
        both = first if both is None else both + first
        down = second if down is None else down + second
    gate_out[...] = both[:, : 2 * LANE].astype(bf16)
    up_out[...] = both[:, 2 * LANE :].astype(bf16)
    down_out[...] = down.astype(bf16)


def weight_grads(core, mine, other, turned, direct):
    rows, wide = mine[0].shape
    depth = direct[0].shape[1] // 2
    tiles = wide // (3 * LANE)
    act = pl.BlockSpec((rows, 3 * LANE), lambda t: (0, t))
    return pl.pallas_call(
        weights_kernel,
        grid=(tiles,),
        in_specs=[pl.BlockSpec(memory_space=pltpu.SMEM)]
        + [act] * 8
        + [pl.BlockSpec(turned[0].shape, lambda t: (0, 0))] * 4
        + [pl.BlockSpec(direct[0].shape, lambda t: (0, 0))] * 4,
        out_specs=[
            pl.BlockSpec((depth, 2 * LANE), lambda t: (0, t)),
            pl.BlockSpec((depth, 2 * LANE), lambda t: (0, t)),
            pl.BlockSpec((2 * LANE, depth), lambda t: (t, 0)),
        ],
        out_shape=[
            jax.ShapeDtypeStruct((depth, tiles * 2 * LANE), bf16),
            jax.ShapeDtypeStruct((depth, tiles * 2 * LANE), bf16),
            jax.ShapeDtypeStruct((tiles * 2 * LANE, depth), bf16),
        ],
        cost_estimate=pl.CostEstimate(
            flops=6 * 4 * rows * depth * tiles * 2 * LANE, bytes_accessed=18000000, transcendentals=0
        ),
        compiler_params=pltpu.CompilerParams(vmem_limit_bytes=40 << 20),
        name="weight_grads",
    )(core, *mine, *other, *turned, *direct)


def local(tokens, out_grad, gate_weight, up_weight, down_weight):
    core = lax.axis_index("core")
    y = lax.axis_index("y")
    xl = lax.axis_index("xl")
    core_ref = jnp.full((1,), core, jnp.int32)
    depth, wide = gate_weight.shape
    tiles = wide // (2 * LANE)

    rows = jnp.concatenate([tokens, out_grad], axis=1)
    width = rows.shape[1]
    rows = rows.reshape(4, 2, 16, width)
    rows = lax.dynamic_slice_in_dim(jnp.concatenate([rows, rows], axis=0), y, 4, axis=0)
    rows = jnp.where(xl == 0, rows, rows[:, ::-1]).reshape(128, width)
    partner = move(rows, "xh", 1)
    pair = jnp.stack([rows.reshape(8, 16, width), partner.reshape(8, 16, width)], axis=1).reshape(256, width)

    def columns(at):
        g = lax.dynamic_index_in_dim(gate_weight.reshape(depth, tiles, 2, LANE), at, 2, keepdims=False)
        u = lax.dynamic_index_in_dim(up_weight.reshape(depth, tiles, 2, LANE), at, 2, keepdims=False)
        d = lax.dynamic_index_in_dim(down_weight.reshape(tiles, 2, LANE, depth), at, 1, keepdims=False)
        return jnp.concatenate([g, u], axis=2).reshape(depth, wide), d.reshape(tiles * LANE, depth)

    gu_own, d_own = columns(core)
    gu_send, d_send = columns(1 - core)
    gu_oth = move(gu_send, "core", 1)
    d_oth = move(d_send, "core", 1)

    pairs = [pair] + [move(pair, "z", by) for by in (3, 1, 2)]
    where = (0, 1, 3, 2)
    others = [move(p, "core", 1) for p in pairs]
    turned = [p.T for p in pairs]

    mine, other, near, far = [], [], [], []
    for k in range(4):
        keep, second, plus, minus = forward(pairs[k], others[k], gu_own, gu_oth, d_own, d_oth)
        from_low = move(plus, "y", 1)
        from_high = move(minus, "y", 3)
        up_sum = (second[0:32] + from_low[32:64].astype(f32)).astype(bf16)
        down_sum = (second[32:64] + from_high[0:32].astype(f32)).astype(bf16)
        second_low = move(up_sum, "y", 1)
        second_high = move(down_sum, "y", 3)
        beside = keep[32:64] + from_low[0:32].astype(f32) + second_high.astype(f32)
        across = move(beside, "xl", 1)
        own = activate(keep, from_high, second_low, across)
        b0 = own
        b1 = move(own, "xl", 1)
        b6 = move(own, "y", 1)
        b2 = move(own, "y", 3)
        b7 = move(b1, "y", 1)
        b3 = move(b1, "y", 3)
        b4 = move(b6, "y", 1)
        b5 = move(b3, "y", 3)
        whole = jnp.concatenate([b0, b1, b2, b3, b4, b5, b6, b7], axis=0)
        mine.append(whole)
        other.append(move(whole, "core", 1))
        n, f = back(core_ref, mine[k], other[k], gate_weight, up_weight, f32 if k == 0 else bf16)
        near.append(n if k == 0 else move(n, "z", where[k]))
        far.append(move2(f, where[k], 1))

    gate_grad, up_grad, down_grad = weight_grads(core_ref, mine, other, turned, pairs)
    total = near[0]
    for part in near[1:] + far:
        total = total + part.astype(f32)
    total = total.astype(bf16).reshape(4, 2, 16, depth)
    total = jnp.where(xl == 0, total, total[:, ::-1])
    total = lax.dynamic_slice_in_dim(jnp.concatenate([total, total], axis=0), (4 - y) % 4, 4, axis=0)
    return total.reshape(128, depth), gate_grad, up_grad, down_grad


def solution(mesh):
    fine = Mesh(mesh.devices.reshape(tuple(AXES.values())), tuple(AXES))
    row, col = ("z", "xh"), ("y", "xl", "core")
    placed = (P(row, col), P(row, col), P(col, row), P(col, row), P(row, col))
    return jax.shard_map(
        local,
        mesh=fine,
        in_specs=placed,
        out_specs=(P(row, col), P(col, row), P(col, row), P(row, col)),
        check_vma=False,
    )
```

```python
import jax
import jax.numpy as jnp
from jax import lax
from jax.experimental import pallas as pl
from jax.experimental.pallas import tpu as pltpu
from jax.sharding import Mesh
from jax.sharding import PartitionSpec as P

AXES = {"z": 4, "xh": 2, "y": 4, "xl": 2, "core": 2}
HALF = 896
D = 512
WIDE = 3 * HALF
f32 = jnp.float32
bf16 = jnp.bfloat16
plain = (((1,), (0,)), ((), ()))
contract_first = (((0,), (0,)), ((), ()))
contract_last = (((1,), (1,)), ((), ()))
vmem = pl.BlockSpec(memory_space=pltpu.VMEM)
anywhere = pl.BlockSpec(memory_space=pl.ANY)
smem = pl.BlockSpec(memory_space=pltpu.SMEM)

AWAY = (0, 1, 2, 3)
ACROSS = f32
ORDER = (
    ("F", 0), ("C", 3), ("C", 1), ("S1", 0), ("F", 3), ("S2", 0), ("F", 1), ("C", 2),
    ("S1", 3), ("ACT", 0), ("S1", 1), ("F", 2), ("S2", 3), ("S2", 1), ("PAIR", 0), ("S1", 2),
    ("ACT", 3), ("S2", 2), ("ACT", 1), ("PAIR", 3), ("ASM", 0), ("ACT", 2), ("PAIR", 1), ("BACK", 0),
    ("ASM", 3), ("PAIR", 2), ("ASM", 1), ("BACK", 3), ("ASM", 2), ("BACK", 1), ("WG", 0), ("BACK", 2),
)


def move(a, axis, by):
    n = AXES[axis]
    return lax.ppermute(a, axis, [(i, (i + by) % n) for i in range(n)])


def move2(a, dz, dx):
    pairs = [(z * 2 + x, ((z + dz) % 4) * 2 + (x + dx) % 2) for z in range(4) for x in range(2)]
    return lax.ppermute(a, ("z", "xh"), pairs)


def step(a, by):
    pairs = [(2 * i, 2 * ((i + by) % 4)) for i in range(4)]
    pairs += [(2 * i + 1, 2 * ((i - by) % 4) + 1) for i in range(4)]
    return lax.ppermute(a, ("y", "core"), pairs)


def dot(a, b, dims):
    return lax.dot_general(a, b, dims, preferred_element_type=f32)


def call(name, body, ids, args, outs, after=(), limit=8, flops=0, scratch=(), in_space=vmem):
    n, m = len(args), len(after)

    def kernel(*refs):
        body(*refs[: 1 + n], *refs[1 + n + m :])

    size = sum(a.size * a.dtype.itemsize for a in args) + sum(
        o.size * jnp.dtype(o.dtype).itemsize for o in outs
    )
    return pl.pallas_call(
        kernel,
        in_specs=[smem] + [in_space] * n + [anywhere] * m,
        out_specs=[vmem] * len(outs),
        out_shape=outs,
        scratch_shapes=scratch,
        cost_estimate=pl.CostEstimate(flops=flops, bytes_accessed=size, transcendentals=0),
        compiler_params=pltpu.CompilerParams(vmem_limit_bytes=limit << 20),
        name=name,
    )(ids, *args, *after)


def shape(rows, cols, dtype=bf16):
    return jax.ShapeDtypeStruct((rows, cols), dtype)


def offset(ids, other=False):
    c = ids[0]
    return pl.multiple_of((1 - c if other else c) * HALF, 128)


def home(ids, b):
    core, y, xl = ids[0], ids[1], ids[2]
    at = (y + 4 + (1 - 2 * core) * (b // 2)) % 4 * 2 + (xl + b % 2) % 2
    return pl.ds(pl.multiple_of(at * 16, 16), 16)


def rows_kernel(ids, tokens, out_grad, out, sems):
    copies = []
    for b in range(8):
        rows = slice(16 * b, 16 * b + 16)
        copies.append(pltpu.make_async_copy(tokens.at[home(ids, b), :], out.at[rows, :D], sems.at[b]))
        copies.append(pltpu.make_async_copy(out_grad.at[home(ids, b), :], out.at[rows, D:], sems.at[8 + b]))
    for c in copies:
        c.start()
    for c in copies:
        c.wait()


def pair_kernel(ids, own, partner, out, turned):
    for b in range(8):
        both = jnp.concatenate([own[16 * b : 16 * b + 16, :], partner[16 * b : 16 * b + 16, :]], axis=0)
        out[32 * b : 32 * b + 32, :] = both
        t = (4 - b // 2) % 4 * 2 + b % 2
        turned[32 * t : 32 * t + 32, :] = both


def turn_kernel(ids, rows, out):
    n = rows.shape[0] // 4
    for j in range(4):
        t = (4 - j) % 4
        out[t * n : t * n + n, :] = rows[j * n : j * n + n, :]


def send_kernel(ids, wg, wu, wd, out, turn, sems):
    at = offset(ids, True)
    copies = [
        pltpu.make_async_copy(wd.at[pl.ds(at, HALF), :], turn, sems.at[0]),
        pltpu.make_async_copy(wg.at[:, pl.ds(at, HALF)], out.at[:, :HALF], sems.at[1]),
        pltpu.make_async_copy(wu.at[:, pl.ds(at, HALF)], out.at[:, HALF : 2 * HALF], sems.at[2]),
    ]
    for c in copies:
        c.start()
    copies[0].wait()
    out[:, 2 * HALF :] = turn[...].T
    copies[1].wait()
    copies[2].wait()


def send_weights(ids, wg, wu, wd, after):
    return pl.pallas_call(
        lambda *r: send_kernel(*r[:4], *r[5:]),
        in_specs=[smem] + [anywhere] * 4,
        out_specs=vmem,
        out_shape=shape(D, WIDE),
        scratch_shapes=[pltpu.VMEM((HALF, D), bf16), pltpu.SemaphoreType.DMA((3,))],
        cost_estimate=pl.CostEstimate(flops=0, bytes_accessed=6 << 20, transcendentals=0),
        compiler_params=pltpu.CompilerParams(vmem_limit_bytes=8 << 20),
        name="send_weights",
    )(ids, wg, wu, wd, after)


def forward_kernel(ids, own, oth, wg, wu, wd, wr, keep, second, far, behind):
    at = offset(ids)
    n = own.shape[0] // 4
    for j in range(3):
        cols = slice(j * HALF, (j + 1) * HALF)
        if j < 2:
            part = dot(own[:, :D], (wg, wu)[j][:, pl.ds(at, HALF)], plain) + dot(
                oth[:, :D], wr[:, cols], plain
            )
        else:
            part = dot(own[:, D:], wd[pl.ds(at, HALF), :], contract_last) + dot(
                oth[:, D:], wr[:, cols], plain
            )
        keep[:, cols] = part[0:n]
        second[:, cols] = part[n : 2 * n]
        far[:, cols] = part[2 * n : 3 * n].astype(bf16)
        behind[:, cols] = part[3 * n :].astype(bf16)


def add_kernel(ids, second, got, out):
    out[...] = (second[...] + got[...].astype(f32)).astype(bf16)


def beside_kernel(ids, keep, ahead, got, out, base):
    u = out.shape[0]
    for rows, dst in ((slice(0, u), base), (slice(u, 2 * u), out)):
        dst[...] = (keep[rows] + ahead[rows].astype(f32) + got[rows].astype(f32)).astype(dst.dtype)


def activate_kernel(ids, base, across, out):
    def total(j):
        cols = slice(j * HALF, (j + 1) * HALF)
        return base[:, cols] + across[:, cols].astype(f32)

    gate, upper, hidden_grad = total(0), total(1), total(2)
    sig = jax.nn.sigmoid(gate)
    silu = gate * sig
    out[:, :HALF] = (silu * upper).astype(bf16)
    out[:, HALF : 2 * HALF] = (hidden_grad * upper * sig * (1.0 + gate * (1.0 - sig))).astype(bf16)
    out[:, 2 * HALF :] = (hidden_grad * silu).astype(bf16)


def both_kernel(ids, a, b, out):
    out[: a.shape[0]] = a[...]
    out[a.shape[0] :] = b[...]


def whole_kernel(ids, p0, p1, p2, p3, out, turned):
    n = p0.shape[0]
    for j, (a, b) in enumerate(((p0, p0), (p1, p3), (p2, p2), (p3, p1))):
        out[n * j : n * j + n] = a[...]
        turned[n * j : n * j + n] = b[...]


def back_kernel(ids, mine, other, wg, wu, near, far):
    a, b = pl.ds(offset(ids), HALF), pl.ds(offset(ids, True), HALF)
    total = dot(mine[:, HALF : 2 * HALF], wg[:, a], contract_last)
    total += dot(mine[:, 2 * HALF :], wu[:, a], contract_last)
    total += dot(other[:, HALF : 2 * HALF], wg[:, b], contract_last)
    total += dot(other[:, 2 * HALF :], wu[:, b], contract_last)
    for k in range(8):
        near[16 * k : 16 * k + 16, :] = total[32 * k : 32 * k + 16].astype(near.dtype)
        far[16 * k : 16 * k + 16, :] = total[32 * k + 16 : 32 * k + 32].astype(far.dtype)


def weights_kernel(n, second, ids, *refs):
    parts, rows, refs = refs[:n], refs[n : 2 * n], refs[2 * n :]
    refs = refs[3:] if second else refs
    gate_out, up_out, down_out, done, gate_buf, up_buf, down_buf, sems = refs
    copies = []

    def put(src, dst, sem):
        copies.append(pltpu.make_async_copy(src, dst, sem))
        copies[-1].start()

    at = pl.ds(offset(ids, second), HALF)
    for j, (out, buf) in enumerate(((gate_out, gate_buf), (up_out, up_buf))):
        total = None
        for p, r in zip(parts, rows):
            term = dot(r[:, :D], p[:, (j + 1) * HALF : (j + 2) * HALF], contract_first)
            total = term if total is None else total + term
        buf[...] = total.astype(bf16)
        put(buf, out.at[:, at], sems.at[j])
    total = None
    for p, r in zip(parts, rows):
        term = dot(p[:, :HALF], r[:, D:], contract_first)
        total = term if total is None else total + term
    down_buf[...] = total.astype(bf16)
    put(down_buf, down_out.at[at, :], sems.at[2])
    done[...] = jnp.zeros_like(done)
    for c in copies:
        c.wait()


def weight_grads(ids, parts, rows, old, after):
    n, second = len(parts), bool(old)
    whole = [shape(D, 2 * HALF), shape(D, 2 * HALF), shape(2 * HALF, D)]

    def kernel(*refs):
        at = 1 + 2 * n + len(old)
        weights_kernel(n, second, *refs[:at], *refs[at + len(after) :])

    return pl.pallas_call(
        kernel,
        in_specs=[smem] + [vmem] * (2 * n) + [anywhere] * (len(old) + len(after)),
        out_specs=[pl.BlockSpec(memory_space=pltpu.HBM)] * 3 + [vmem],
        out_shape=whole + [shape(8, 128, f32)],
        input_output_aliases={1 + 2 * n + i: i for i in range(len(old))},
        scratch_shapes=[pltpu.VMEM((D, HALF), bf16)] * 2 + [pltpu.VMEM((HALF, D), bf16), pltpu.SemaphoreType.DMA((3,))],
        cost_estimate=pl.CostEstimate(flops=6 * 1024 * D * HALF, bytes_accessed=10 << 20, transcendentals=0),
        compiler_params=pltpu.CompilerParams(vmem_limit_bytes=24 << 20),
        name="weight_grads",
    )(ids, *parts, *rows, *old, *after)


def sum_kernel(ids, *refs):
    out = refs[-1]
    for b in range(8):
        rows = slice(16 * b, 16 * b + 16)
        total = refs[0][rows, :].astype(f32)
        for r in refs[1:-1]:
            total = total + r[rows, :].astype(f32)
        out[home(ids, b), :] = total.astype(bf16)


def local(tokens, out_grad, wg, wu, wd):
    ids = jnp.stack([lax.axis_index(a) for a in ("core", "y", "xl")]).astype(jnp.int32)

    (rows,) = call(
        "rows", rows_kernel, ids, [tokens, out_grad], [shape(128, 2 * D)],
        scratch=[pltpu.SemaphoreType.DMA((16,))], in_space=anywhere,
    )
    partner = move(rows, "xh", 1)
    wr = move(send_weights(ids, wg, wu, wd, rows), "core", 1)
    pair, turned = call("pair", pair_kernel, ids, [rows, partner], [shape(256, 2 * D)] * 2, flops=20 << 30)
    oth = {0: move(turned, "core", 1)}
    own = {0: pair, 1: move(pair, "z", 3), 3: move(pair, "z", 1), 2: move(pair, "z", 2)}

    n = len(AWAY)
    st = [{} for _ in range(n)]
    last = ()
    near, far = [], []
    for stage, k in ORDER:
        s = st[k]
        count = own[k].shape[0]
        u = count // 8
        if stage == "C":
            outs = call("turn", turn_kernel, ids, [own[k]], [shape(count, 2 * D)], last)
            oth[k] = move(outs[0], "core", 1)
        elif stage == "F":
            outs = call(
                "forward", forward_kernel, ids, [own[k], oth[k], wg, wu, wd, wr],
                [shape(2 * u, WIDE, f32)] * 2 + [shape(2 * u, WIDE)] * 2, last, limit=24, flops=4 * count * D * WIDE,
            )
            s["keep"], s["second"] = outs[:2]
            s["got"], s["ahead"] = step(outs[2], 1), step(outs[3], -1)
        elif stage == "S1":
            outs = call("add", add_kernel, ids, [s["second"], s["got"]], [shape(2 * u, WIDE)], last)
            s["got2"] = step(outs[0], 1)
        elif stage == "S2":
            outs = call(
                "beside", beside_kernel, ids, [s["keep"], s["ahead"], s["got2"]],
                [shape(u, WIDE, ACROSS), shape(u, WIDE, f32)], last,
            )
            s["across"], s["base"] = move(outs[0], "xl", 1), outs[1]
        elif stage == "ACT":
            outs = call("activate", activate_kernel, ids, [s["base"], s["across"]], [shape(u, WIDE)], last)
            s["b0"], s["b1"] = outs[0], move(outs[0], "xl", 1)
        elif stage == "PAIR":
            outs = call("both", both_kernel, ids, [s["b0"], s["b1"]], [shape(2 * u, WIDE)], last)
            s["p0"] = outs[0]
            s["p3"], s["p1"] = step(outs[0], 1), step(outs[0], -1)
            s["p2"] = step(s["p3"], 1)
        elif stage == "ASM":
            parts = [s["p0"], s["p1"], s["p2"], s["p3"]]
            outs = call("whole", whole_kernel, ids, parts, [shape(count, WIDE)] * 2, last)
            s["mine"], s["other"] = outs[0], move(outs[1], "core", 1)
        elif stage == "WG":
            grads = weight_grads(ids, [s["mine"] for s in st], [own[k] for k in range(n)], (), last)
            outs = (grads[3],)
        else:
            last += tuple(near[-1:] + far[-1:])
            outs = call(
                "back", back_kernel, ids, [s["mine"], s["other"], wg, wu],
                [shape(128, D, f32 if AWAY[k] == 0 else bf16), shape(128, D)],
                last, limit=16, flops=8 * count * D * HALF,
            )
            near.append(outs[0] if AWAY[k] == 0 else move(outs[0], "z", AWAY[k]))
            far.append(move2(outs[1], AWAY[k], 1))
        last = (outs[0],)

    rest = weight_grads(ids, [s["other"] for s in st], [own[k] for k in range(n)], grads[:3], last)
    gate_grad, up_grad, down_grad, done = rest
    (tokens_grad,) = call("total", sum_kernel, ids, near + far, [shape(128, D)], (done,))
    return tokens_grad, gate_grad, up_grad, down_grad


def solution(mesh):
    fine = Mesh(mesh.devices.reshape(tuple(AXES.values())), tuple(AXES))
    row, col = ("z", "xh"), ("y", "xl", "core")
    placed = (P(row, col), P(row, col), P(col, row), P(col, row), P(row, col))
    return jax.shard_map(
        local,
        mesh=fine,
        in_specs=placed,
        out_specs=(P(row, col), P(col, row), P(col, row), P(row, col)),
        check_vma=False,
    )
```

```python
import jax
import jax.numpy as jnp
from jax import lax
from jax.experimental import pallas as pl
from jax.experimental.pallas import tpu as pltpu
from jax.sharding import Mesh
from jax.sharding import PartitionSpec as P

AXES = {"z": 4, "xh": 2, "y": 4, "xl": 2, "core": 2}
HALF = 896
D = 512
WIDE = 3 * HALF
f32 = jnp.float32
bf16 = jnp.bfloat16
plain = (((1,), (0,)), ((), ()))
contract_first = (((0,), (0,)), ((), ()))
contract_last = (((1,), (1,)), ((), ()))
vmem = pl.BlockSpec(memory_space=pltpu.VMEM)
anywhere = pl.BlockSpec(memory_space=pl.ANY)
hbm = pl.BlockSpec(memory_space=pltpu.HBM)
smem = pl.BlockSpec(memory_space=pltpu.SMEM)

CHUNKS = ((0,), (3,), (1,), (2,))
GROUPS = ((0,), (1,), (2,), (3,))
LAG = 3
ORDER = (
    ("F", 0), ("C", 1), ("C", 2), ("S1", 0), ("F", 1), ("S2", 0), ("F", 2), ("C", 3),
    ("S1", 1), ("ACT", 0), ("S1", 2), ("F", 3), ("S2", 1), ("S2", 2), ("S1", 3), ("ACT", 1),
    ("S2", 3), ("ASM", 0), ("ACT", 2), ("ASM", 1), ("BACK", 0), ("ACT", 3), ("ASM", 2), ("BACK", 1),
    ("ASM", 3), ("BACK", 2), ("WG", 0), ("BACK", 3),
)


def move(a, axis, by):
    n = AXES[axis]
    return lax.ppermute(a, axis, [(i, (i + by) % n) for i in range(n)])


def move2(a, dz, dx):
    pairs = [(z * 2 + x, ((z + dz) % 4) * 2 + (x + dx) % 2) for z in range(4) for x in range(2)]
    return lax.ppermute(a, ("z", "xh"), pairs)


def step(a, by):
    pairs = [(2 * i, 2 * ((i + by) % 4)) for i in range(4)]
    pairs += [(2 * i + 1, 2 * ((i - by) % 4) + 1) for i in range(4)]
    return lax.ppermute(a, ("y", "core"), pairs)


def dot(a, b, dims):
    return lax.dot_general(a, b, dims, preferred_element_type=f32)


def call(name, body, ids, args, outs, after=(), limit=8, flops=0, scratch=(), in_space=vmem):
    n, m = len(args), len(after)

    def kernel(*refs):
        body(*refs[: 1 + n], *refs[1 + n + m :])

    size = sum(a.size * a.dtype.itemsize for a in args) + sum(
        o.size * jnp.dtype(o.dtype).itemsize for o in outs
    )
    return pl.pallas_call(
        kernel,
        in_specs=[smem] + [in_space] * n + [anywhere] * m,
        out_specs=[vmem] * len(outs),
        out_shape=outs,
        scratch_shapes=scratch,
        cost_estimate=pl.CostEstimate(flops=flops if name == "pair" else 0, bytes_accessed=0, transcendentals=0),
        compiler_params=pltpu.CompilerParams(vmem_limit_bytes=limit << 20),
        name=name,
    )(ids, *args, *after)


def shape(rows, cols, dtype=bf16):
    return jax.ShapeDtypeStruct((rows, cols), dtype)


def offset(ids, other=False):
    c = ids[0]
    return pl.multiple_of((1 - c if other else c) * HALF, 128)


def home(ids, b):
    core, y, xl = ids[0], ids[1], ids[2]
    at = (y + 4 + (1 - 2 * core) * (b // 2)) % 4 * 2 + (xl + b % 2) % 2
    return pl.ds(pl.multiple_of(at * 16, 16), 16)


def rows_kernel(ids, tokens, out_grad, out, sems):
    copies = []
    for b in range(8):
        rows = slice(16 * b, 16 * b + 16)
        copies.append(pltpu.make_async_copy(tokens.at[home(ids, b), :], out.at[rows, :D], sems.at[b]))
        copies.append(pltpu.make_async_copy(out_grad.at[home(ids, b), :], out.at[rows, D:], sems.at[8 + b]))
    for c in copies:
        c.start()
    for c in copies:
        c.wait()


def pair_kernel(ids, own, partner, out, turned):
    for b in range(8):
        both = jnp.concatenate([own[16 * b : 16 * b + 16, :], partner[16 * b : 16 * b + 16, :]], axis=0)
        out[32 * b : 32 * b + 32, :] = both
        t = (4 - b // 2) % 4 * 2 + b % 2
        turned[32 * t : 32 * t + 32, :] = both


def turn_kernel(ids, *refs):
    parts, (out, turned) = refs[:-2], refs[-2:]
    n = len(parts)
    for b in range(8):
        t = (4 - b // 2) % 4 * 2 + b % 2
        for m, p in enumerate(parts):
            rows = p[32 * b : 32 * b + 32, :]
            at = 32 * (n * b + m)
            out[at : at + 32, :] = rows
            at = 32 * (n * t + m)
            turned[at : at + 32, :] = rows


def send_kernel(ids, wg, wu, wd, out, turn, sems):
    at = offset(ids, True)
    copies = [
        pltpu.make_async_copy(wd.at[pl.ds(at, HALF), :], turn, sems.at[0]),
        pltpu.make_async_copy(wg.at[:, pl.ds(at, HALF)], out.at[:, :HALF], sems.at[1]),
        pltpu.make_async_copy(wu.at[:, pl.ds(at, HALF)], out.at[:, HALF : 2 * HALF], sems.at[2]),
    ]
    for c in copies:
        c.start()
    copies[0].wait()
    out[:, 2 * HALF :] = turn[...].T
    copies[1].wait()
    copies[2].wait()


def send_weights(ids, wg, wu, wd, after):
    return pl.pallas_call(
        lambda *r: send_kernel(*r[:4], *r[5:]),
        in_specs=[smem] + [hbm] * 3 + [anywhere],
        out_specs=vmem,
        out_shape=shape(D, WIDE),
        scratch_shapes=[pltpu.VMEM((HALF, D), bf16), pltpu.SemaphoreType.DMA((3,))],
        cost_estimate=pl.CostEstimate(flops=0, bytes_accessed=6 << 20, transcendentals=0),
        compiler_params=pltpu.CompilerParams(vmem_limit_bytes=8 << 20),
        name="send_weights",
    )(ids, wg, wu, wd, after)


def forward_kernel(ids, own, oth, wg, wu, wd, wr, keep, second, far, behind):
    at = offset(ids)
    n = own.shape[0] // 4
    for j in range(3):
        cols = slice(j * HALF, (j + 1) * HALF)
        if j < 2:
            part = dot(own[:, :D], (wg, wu)[j][:, pl.ds(at, HALF)], plain) + dot(
                oth[:, :D], wr[:, cols], plain
            )
        else:
            part = dot(own[:, D:], wd[pl.ds(at, HALF), :], contract_last) + dot(
                oth[:, D:], wr[:, cols], plain
            )
        keep[:, cols] = part[0:n]
        second[:, cols] = part[n : 2 * n]
        far[:, cols] = part[2 * n : 3 * n].astype(bf16)
        behind[:, cols] = part[3 * n :].astype(bf16)


def add_kernel(ids, second, got, out):
    out[...] = (second[...] + got[...].astype(f32)).astype(bf16)


def beside_kernel(ids, keep, ahead, got, out):
    out[...] = keep[...] + ahead[...].astype(f32) + got[...].astype(f32)


def activate_kernel(ids, base, across, out):
    u = out.shape[0] // 2
    for h in range(2):
        mine, theirs = slice(h * u, h * u + u), slice((1 - h) * u, (1 - h) * u + u)

        def total(j):
            cols = slice(j * HALF, (j + 1) * HALF)
            return base[mine, cols] + across[theirs, cols].astype(f32)

        gate, upper, hidden_grad = total(0), total(1), total(2)
        sig = jax.nn.sigmoid(gate)
        silu = gate * sig
        out[mine, :HALF] = (silu * upper).astype(bf16)
        out[mine, HALF : 2 * HALF] = (hidden_grad * upper * sig * (1.0 + gate * (1.0 - sig))).astype(bf16)
        out[mine, 2 * HALF :] = (hidden_grad * silu).astype(bf16)


def whole_kernel(sizes, ids, p0, p1, p2, p3, out, turned):
    at = 0
    for n in sizes:
        for j, (a, b) in enumerate(((p0, p0), (p1, p3), (p2, p2), (p3, p1))):
            dst = slice(4 * at + n * j, 4 * at + n * j + n)
            out[dst] = a[at : at + n]
            turned[dst] = b[at : at + n]
        at += n


def back_kernel(parts, ids, mine, other, wg, wu, *outs):
    a, b = pl.ds(offset(ids), HALF), pl.ds(offset(ids, True), HALF)
    total = dot(mine[:, HALF : 2 * HALF], wg[:, a], contract_last)
    total += dot(mine[:, 2 * HALF :], wu[:, a], contract_last)
    total += dot(other[:, HALF : 2 * HALF], wg[:, b], contract_last)
    total += dot(other[:, 2 * HALF :], wu[:, b], contract_last)
    for i, (at, apart) in enumerate(parts):
        near, far = outs[2 * i : 2 * i + 2]
        for k in range(8):
            rows = at + apart * k
            near[16 * k : 16 * k + 16, :] = total[rows : rows + 16].astype(near.dtype)
            far[16 * k : 16 * k + 16, :] = total[rows + 16 : rows + 32].astype(far.dtype)


def weights_kernel(n, groups, second, ids, *refs):
    whole, rows, refs = refs[: len(groups)], refs[len(groups) : len(groups) + n], refs[len(groups) + n :]
    parts = []
    for w, group in zip(whole, groups):
        at = 0
        for i in group:
            parts.append(w.at[at : at + rows[i].shape[0]])
            at += rows[i].shape[0]
    rows = [rows[i] for group in groups for i in group]
    refs = refs[3:] if second else refs
    gate_out, up_out, down_out, done, gate_buf, up_buf, down_buf, sems = refs
    copies = []

    def put(src, dst, sem):
        copies.append(pltpu.make_async_copy(src, dst, sem))
        copies[-1].start()

    at = pl.ds(offset(ids, second), HALF)
    for j, (out, buf) in enumerate(((gate_out, gate_buf), (up_out, up_buf))):
        total = None
        for p, r in zip(parts, rows):
            term = dot(r[:, :D], p[:, (j + 1) * HALF : (j + 2) * HALF], contract_first)
            total = term if total is None else total + term
        buf[...] = total.astype(bf16)
        put(buf, out.at[:, at], sems.at[j])
    total = None
    for p, r in zip(parts, rows):
        term = dot(p[:, :HALF], r[:, D:], contract_first)
        total = term if total is None else total + term
    down_buf[...] = total.astype(bf16)
    put(down_buf, down_out.at[at, :], sems.at[2])
    done[...] = jnp.zeros_like(done)
    for c in copies:
        c.wait()


def weight_grads(ids, parts, rows, old, after):
    n, second = len(rows), bool(old)
    given = len(parts) + n
    whole = [shape(D, 2 * HALF), shape(D, 2 * HALF), shape(2 * HALF, D)]

    def kernel(*refs):
        at = 1 + given + len(old)
        weights_kernel(n, GROUPS, second, *refs[:at], *refs[at + len(after) :])

    return pl.pallas_call(
        kernel,
        in_specs=[smem] + [vmem] * given + [anywhere] * (len(old) + len(after)),
        out_specs=[hbm] * 3 + [vmem],
        out_shape=whole + [shape(8, 128, f32)],
        input_output_aliases={1 + given + i: i for i in range(len(old))},
        scratch_shapes=[pltpu.VMEM((D, HALF), bf16)] * 2 + [pltpu.VMEM((HALF, D), bf16), pltpu.SemaphoreType.DMA((3,))],
        cost_estimate=pl.CostEstimate(flops=0, bytes_accessed=0, transcendentals=0),
        compiler_params=pltpu.CompilerParams(vmem_limit_bytes=24 << 20),
        name="weight_grads",
    )(ids, *parts, *rows, *old, *after)


def sum_kernel(ids, *refs):
    out = refs[-1]
    for b in range(8):
        rows = slice(16 * b, 16 * b + 16)
        total = refs[0][rows, :].astype(f32)
        for r in refs[1:-1]:
            total = total + r[rows, :].astype(f32)
        out[home(ids, b), :] = total.astype(bf16)


def local(tokens, out_grad, wg, wu, wd):
    ids = jnp.stack([lax.axis_index(a) for a in ("core", "y", "xl")]).astype(jnp.int32)

    (rows,) = call(
        "rows", rows_kernel, ids, [tokens, out_grad], [shape(128, 2 * D)],
        scratch=[pltpu.SemaphoreType.DMA((16,))], in_space=hbm,
    )
    partner = move(rows, "xh", 1)
    wr = move(send_weights(ids, wg, wu, wd, rows), "core", 1)
    pair, turned = call("pair", pair_kernel, ids, [rows, partner], [shape(256, 2 * D)] * 2, flops=20 << 30)
    placed = {0: pair, 1: move(pair, "z", 3), 3: move(pair, "z", 1), 2: move(pair, "z", 2)}
    own, oth = {0: pair}, {0: move(turned, "core", 1)}

    n = len(CHUNKS)
    st = [{} for _ in range(n)]
    gr = [{} for _ in GROUPS]
    last = ()
    near, far, due = [], [], []
    for at, (stage, k) in enumerate(ORDER):
        if due and due[0][0] == at:
            last += due.pop(0)[1]
        if stage in ("C", "F", "S1", "S2", "ACT"):
            s = st[k]
            u = 32 * len(CHUNKS[k])
        else:
            s = gr[k]
            us = [32 * len(CHUNKS[i]) for i in GROUPS[k]]
            count = 8 * sum(us)
        if stage == "C":
            parts = [placed[a] for a in CHUNKS[k]]
            outs = call("turn", turn_kernel, ids, parts, [shape(8 * u, 2 * D)] * 2, last)
            own[k], oth[k] = outs[0], move(outs[1], "core", 1)
        elif stage == "F":
            outs = call(
                "forward", forward_kernel, ids, [own[k], oth[k], wg, wu, wd, wr],
                [shape(2 * u, WIDE, f32)] * 2 + [shape(2 * u, WIDE)] * 2, last, limit=32, flops=32 * u * D * WIDE,
            )
            s["keep"], s["second"] = outs[:2]
            s["got"], s["ahead"] = step(outs[2], 1), step(outs[3], -1)
        elif stage == "S1":
            outs = call("add", add_kernel, ids, [s["second"], s["got"]], [shape(2 * u, WIDE)], last)
            s["got2"] = step(outs[0], 1)
        elif stage == "S2":
            outs = call(
                "beside", beside_kernel, ids, [s["keep"], s["ahead"], s["got2"]],
                [shape(2 * u, WIDE, f32)], last,
            )
            s["across"], s["base"] = move(outs[0], "xl", 1), outs[0]
        elif stage == "ACT":
            outs = call("activate", activate_kernel, ids, [s["base"], s["across"]], [shape(2 * u, WIDE)], last)
            s = gr[k]
            s["p0"] = outs[0]
            s["p3"], s["p1"] = step(outs[0], 1), step(outs[0], -1)
            s["p2"] = step(s["p3"], 1)
        elif stage == "ASM":
            parts = [s["p0"], s["p1"], s["p2"], s["p3"]]
            sizes = [2 * u for u in us]
            outs = call(
                "whole", lambda *r, sizes=sizes: whole_kernel(sizes, *r), ids, parts, [shape(count, WIDE)] * 2, last, limit=16
            )
            s["mine"], s["other"] = outs[0], move(outs[1], "core", 1)
        elif stage == "WG":
            grads = weight_grads(ids, [g["mine"] for g in gr], [own[i] for i in range(n)], (), last)
            outs = (grads[3],)
        else:
            parts, owners, start = [], [], 0
            for i in GROUPS[k]:
                for m, a in enumerate(CHUNKS[i]):
                    parts.append((start + 32 * m, 32 * len(CHUNKS[i])))
                    owners.append(a)
                start += 256 * len(CHUNKS[i])
            outs = call(
                "back", lambda *r, parts=parts: back_kernel(parts, *r), ids, [s["mine"], s["other"], wg, wu],
                [shape(128, D, f32 if a == 0 and x == 0 else bf16) for a in owners for x in (0, 1)],
                last, limit=24, flops=8 * count * D * HALF,
            )
            sent = ()
            for i, a in enumerate(owners):
                near.append(outs[2 * i] if a == 0 else move(outs[2 * i], "z", a))
                far.append(move2(outs[2 * i + 1], a, 1))
                sent += (far[-1],) if a == 0 else (near[-1], far[-1])
            due.append((at + LAG, sent))
        last = (outs[0],)

    rest = weight_grads(ids, [g["other"] for g in gr], [own[i] for i in range(n)], grads[:3], last)
    gate_grad, up_grad, down_grad, done = rest
    (tokens_grad,) = call("total", sum_kernel, ids, near + far, [shape(128, D)], (done,))
    return tokens_grad, gate_grad, up_grad, down_grad


def solution(mesh):
    fine = Mesh(mesh.devices.reshape(tuple(AXES.values())), tuple(AXES))
    row, col = ("z", "xh"), ("y", "xl", "core")
    placed = (P(row, col), P(row, col), P(col, row), P(col, row), P(row, col))
    return jax.shard_map(
        local,
        mesh=fine,
        in_specs=placed,
        out_specs=(P(row, col), P(col, row), P(col, row), P(row, col)),
        check_vma=False,
    )
```

```python
import jax
import jax.numpy as jnp
from jax import lax
from jax.experimental import pallas as pl
from jax.experimental.pallas import tpu as pltpu
from jax.sharding import Mesh
from jax.sharding import PartitionSpec as P

AXES = {"z": 4, "xh": 2, "y": 4, "xl": 2, "core": 2}
HALF = 896
D = 512
WIDE = 3 * HALF
f32 = jnp.float32
bf16 = jnp.bfloat16
plain = (((1,), (0,)), ((), ()))
contract_first = (((0,), (0,)), ((), ()))
contract_last = (((1,), (1,)), ((), ()))
vmem = pl.BlockSpec(memory_space=pltpu.VMEM)
anywhere = pl.BlockSpec(memory_space=pl.ANY)
hbm = pl.BlockSpec(memory_space=pltpu.HBM)
smem = pl.BlockSpec(memory_space=pltpu.SMEM)

CHUNKS = ((0,), (3,), (1,), (2,))
GROUPS = ((0,), (1,), (2,), (3,))
ORDER = (
    ("F", 0), ("C", 1), ("C", 2), ("S1", 0), ("F", 1), ("S2", 0), ("F", 2), ("C", 3),
    ("S1", 1), ("ACT", 0), ("S1", 2), ("F", 3), ("S2", 1), ("S2", 2), ("S1", 3), ("ACT", 1),
    ("S2", 3), ("ASM", 0), ("ACT", 2), ("ASM", 1), ("BACK", 0), ("ACT", 3), ("ASM", 2), ("BACK", 1),
    ("ASM", 3), ("BACK", 2), ("BACK", 3), ("WG", 0),
)


def move(a, axis, by):
    n = AXES[axis]
    return lax.ppermute(a, axis, [(i, (i + by) % n) for i in range(n)])


def move2(a, dz, dx):
    pairs = [(z * 2 + x, ((z + dz) % 4) * 2 + (x + dx) % 2) for z in range(4) for x in range(2)]
    return lax.ppermute(a, ("z", "xh"), pairs)


def step(a, by):
    pairs = [(2 * i, 2 * ((i + by) % 4)) for i in range(4)]
    pairs += [(2 * i + 1, 2 * ((i - by) % 4) + 1) for i in range(4)]
    return lax.ppermute(a, ("y", "core"), pairs)


def dot(a, b, dims):
    return lax.dot_general(a, b, dims, preferred_element_type=f32)


def call(name, body, ids, args, outs, after=(), limit=8, flops=0, scratch=(), in_space=vmem):
    n, m = len(args), len(after)

    def kernel(*refs):
        body(*refs[: 1 + n], *refs[1 + n + m :])

    size = sum(a.size * a.dtype.itemsize for a in args) + sum(
        o.size * jnp.dtype(o.dtype).itemsize for o in outs
    )
    return pl.pallas_call(
        kernel,
        in_specs=[smem] + [in_space] * n + [anywhere] * m,
        out_specs=[vmem] * len(outs),
        out_shape=outs,
        scratch_shapes=scratch,
        cost_estimate=pl.CostEstimate(flops=flops if name == "pair" else 0, bytes_accessed=0, transcendentals=0),
        compiler_params=pltpu.CompilerParams(vmem_limit_bytes=limit << 20),
        name=name,
    )(ids, *args, *after)


def shape(rows, cols, dtype=bf16):
    return jax.ShapeDtypeStruct((rows, cols), dtype)


def offset(ids, other=False):
    c = ids[0]
    return pl.multiple_of((1 - c if other else c) * HALF, 128)


def home(ids, b):
    core, y, xl = ids[0], ids[1], ids[2]
    at = (y + 4 + (1 - 2 * core) * (b // 2)) % 4 * 2 + (xl + b % 2) % 2
    return pl.ds(pl.multiple_of(at * 16, 16), 16)


def rows_kernel(ids, tokens, out_grad, out, sems):
    copies = []
    for b in range(8):
        rows = slice(16 * b, 16 * b + 16)
        copies.append(pltpu.make_async_copy(tokens.at[home(ids, b), :], out.at[rows, :D], sems.at[b]))
        copies.append(pltpu.make_async_copy(out_grad.at[home(ids, b), :], out.at[rows, D:], sems.at[8 + b]))
    for c in copies:
        c.start()
    for c in copies:
        c.wait()


def pair_kernel(ids, own, partner, out, turned):
    for b in range(8):
        both = jnp.concatenate([own[16 * b : 16 * b + 16, :], partner[16 * b : 16 * b + 16, :]], axis=0)
        out[32 * b : 32 * b + 32, :] = both
        t = (4 - b // 2) % 4 * 2 + b % 2
        turned[32 * t : 32 * t + 32, :] = both


def turn_kernel(ids, *refs):
    parts, (out, turned) = refs[:-2], refs[-2:]
    n = len(parts)
    for b in range(8):
        t = (4 - b // 2) % 4 * 2 + b % 2
        for m, p in enumerate(parts):
            rows = p[32 * b : 32 * b + 32, :]
            at = 32 * (n * b + m)
            out[at : at + 32, :] = rows
            at = 32 * (n * t + m)
            turned[at : at + 32, :] = rows


def send_kernel(ids, wg, wu, wd, out, turn, sems):
    at = offset(ids, True)
    copies = [
        pltpu.make_async_copy(wd.at[pl.ds(at, HALF), :], turn, sems.at[0]),
        pltpu.make_async_copy(wg.at[:, pl.ds(at, HALF)], out.at[:, :HALF], sems.at[1]),
        pltpu.make_async_copy(wu.at[:, pl.ds(at, HALF)], out.at[:, HALF : 2 * HALF], sems.at[2]),
    ]
    for c in copies:
        c.start()
    copies[0].wait()
    out[:, 2 * HALF :] = turn[...].T
    copies[1].wait()
    copies[2].wait()


def send_weights(ids, wg, wu, wd, after):
    return pl.pallas_call(
        lambda *r: send_kernel(*r[:4], *r[5:]),
        in_specs=[smem] + [hbm] * 3 + [anywhere],
        out_specs=vmem,
        out_shape=shape(D, WIDE),
        scratch_shapes=[pltpu.VMEM((HALF, D), bf16), pltpu.SemaphoreType.DMA((3,))],
        cost_estimate=pl.CostEstimate(flops=0, bytes_accessed=6 << 20, transcendentals=0),
        compiler_params=pltpu.CompilerParams(vmem_limit_bytes=8 << 20),
        name="send_weights",
    )(ids, wg, wu, wd, after)


def forward_kernel(ids, own, oth, wg, wu, wd, wr, keep, second, far, behind):
    at = offset(ids)
    n = own.shape[0] // 4
    for j in range(3):
        cols = slice(j * HALF, (j + 1) * HALF)
        if j < 2:
            part = dot(own[:, :D], (wg, wu)[j][:, pl.ds(at, HALF)], plain) + dot(
                oth[:, :D], wr[:, cols], plain
            )
        else:
            part = dot(own[:, D:], wd[pl.ds(at, HALF), :], contract_last) + dot(
                oth[:, D:], wr[:, cols], plain
            )
        keep[:, cols] = part[0:n]
        second[:, cols] = part[n : 2 * n]
        far[:, cols] = part[2 * n : 3 * n].astype(bf16)
        behind[:, cols] = part[3 * n :].astype(bf16)


def add_kernel(ids, second, got, out):
    out[...] = (second[...] + got[...].astype(f32)).astype(bf16)


def beside_kernel(ids, keep, ahead, got, out):
    out[...] = keep[...] + ahead[...].astype(f32) + got[...].astype(f32)


def activate_kernel(ids, base, across, out):
    u = out.shape[0] // 2
    for h in range(2):
        mine, theirs = slice(h * u, h * u + u), slice((1 - h) * u, (1 - h) * u + u)

        def total(j):
            cols = slice(j * HALF, (j + 1) * HALF)
            return base[mine, cols] + across[theirs, cols].astype(f32)

        gate, upper, hidden_grad = total(0), total(1), total(2)
        sig = jax.nn.sigmoid(gate)
        silu = gate * sig
        out[mine, :HALF] = (silu * upper).astype(bf16)
        out[mine, HALF : 2 * HALF] = (hidden_grad * upper * sig * (1.0 + gate * (1.0 - sig))).astype(bf16)
        out[mine, 2 * HALF :] = (hidden_grad * silu).astype(bf16)


def whole_kernel(sizes, ids, p0, p1, p2, p3, out, turned):
    at = 0
    for n in sizes:
        for j, (a, b) in enumerate(((p0, p0), (p1, p3), (p2, p2), (p3, p1))):
            dst = slice(4 * at + n * j, 4 * at + n * j + n)
            out[dst] = a[at : at + n]
            turned[dst] = b[at : at + n]
        at += n


def back_kernel(parts, ids, mine, other, wg, wu, *outs):
    a, b = pl.ds(offset(ids), HALF), pl.ds(offset(ids, True), HALF)
    total = dot(mine[:, HALF : 2 * HALF], wg[:, a], contract_last)
    total += dot(mine[:, 2 * HALF :], wu[:, a], contract_last)
    total += dot(other[:, HALF : 2 * HALF], wg[:, b], contract_last)
    total += dot(other[:, 2 * HALF :], wu[:, b], contract_last)
    for i, (at, apart) in enumerate(parts):
        near, far = outs[2 * i : 2 * i + 2]
        for k in range(8):
            rows = at + apart * k
            near[16 * k : 16 * k + 16, :] = total[rows : rows + 16].astype(near.dtype)
            far[16 * k : 16 * k + 16, :] = total[rows + 16 : rows + 32].astype(far.dtype)


def weights_kernel(n, groups, second, ids, *refs):
    whole, rows, refs = refs[: len(groups)], refs[len(groups) : len(groups) + n], refs[len(groups) + n :]
    parts = []
    for w, group in zip(whole, groups):
        at = 0
        for i in group:
            parts.append(w.at[at : at + rows[i].shape[0]])
            at += rows[i].shape[0]
    rows = [rows[i] for group in groups for i in group]
    refs = refs[3:] if second else refs
    gate_out, up_out, down_out, done, gate_buf, up_buf, down_buf, sems = refs
    copies = []

    def put(src, dst, sem):
        copies.append(pltpu.make_async_copy(src, dst, sem))
        copies[-1].start()

    at = pl.ds(offset(ids, second), HALF)
    for j, (out, buf) in enumerate(((gate_out, gate_buf), (up_out, up_buf))):
        total = None
        for p, r in zip(parts, rows):
            term = dot(r[:, :D], p[:, (j + 1) * HALF : (j + 2) * HALF], contract_first)
            total = term if total is None else total + term
        buf[...] = total.astype(bf16)
        put(buf, out.at[:, at], sems.at[j])
    total = None
    for p, r in zip(parts, rows):
        term = dot(p[:, :HALF], r[:, D:], contract_first)
        total = term if total is None else total + term
    down_buf[...] = total.astype(bf16)
    put(down_buf, down_out.at[at, :], sems.at[2])
    done[...] = jnp.zeros_like(done)
    for c in copies:
        c.wait()


def weight_grads(ids, parts, rows, old, after):
    n, second = len(rows), bool(old)
    given = len(parts) + n
    whole = [shape(D, 2 * HALF), shape(D, 2 * HALF), shape(2 * HALF, D)]

    def kernel(*refs):
        at = 1 + given + len(old)
        weights_kernel(n, GROUPS, second, *refs[:at], *refs[at + len(after) :])

    return pl.pallas_call(
        kernel,
        in_specs=[smem] + [vmem] * given + [anywhere] * (len(old) + len(after)),
        out_specs=[hbm] * 3 + [vmem],
        out_shape=whole + [shape(8, 128, f32)],
        input_output_aliases={1 + given + i: i for i in range(len(old))},
        scratch_shapes=[pltpu.VMEM((D, HALF), bf16)] * 2 + [pltpu.VMEM((HALF, D), bf16), pltpu.SemaphoreType.DMA((3,))],
        cost_estimate=pl.CostEstimate(flops=0, bytes_accessed=0, transcendentals=0),
        compiler_params=pltpu.CompilerParams(vmem_limit_bytes=24 << 20),
        name="weight_grads",
    )(ids, *parts, *rows, *old, *after)


def sum_kernel(ids, *refs):
    out = refs[-1]
    for b in range(8):
        rows = slice(16 * b, 16 * b + 16)
        total = refs[0][rows, :].astype(f32)
        for r in refs[1:-1]:
            total = total + r[rows, :].astype(f32)
        out[home(ids, b), :] = total.astype(bf16)


def local(tokens, out_grad, wg, wu, wd):
    ids = jnp.stack([lax.axis_index(a) for a in ("core", "y", "xl")]).astype(jnp.int32)

    (rows,) = call(
        "rows", rows_kernel, ids, [tokens, out_grad], [shape(128, 2 * D)],
        scratch=[pltpu.SemaphoreType.DMA((16,))], in_space=hbm,
    )
    partner = move(rows, "xh", 1)
    wr = move(send_weights(ids, wg, wu, wd, rows), "core", 1)
    pair, turned = call("pair", pair_kernel, ids, [rows, partner], [shape(256, 2 * D)] * 2, flops=20 << 30)
    placed = {0: pair, 1: move(pair, "z", 3), 3: move(pair, "z", 1), 2: move(pair, "z", 2)}
    own, oth = {0: pair}, {0: move(turned, "core", 1)}

    n = len(CHUNKS)
    st = [{} for _ in range(n)]
    gr = [{} for _ in GROUPS]
    last = ()
    near, far = [], []
    for stage, k in ORDER:
        if stage in ("C", "F", "S1", "S2", "ACT"):
            s = st[k]
            u = 32 * len(CHUNKS[k])
        else:
            s = gr[k]
            us = [32 * len(CHUNKS[i]) for i in GROUPS[k]]
            count = 8 * sum(us)
        if stage == "C":
            parts = [placed[a] for a in CHUNKS[k]]
            outs = call("turn", turn_kernel, ids, parts, [shape(8 * u, 2 * D)] * 2, last)
            own[k], oth[k] = outs[0], move(outs[1], "core", 1)
        elif stage == "F":
            outs = call(
                "forward", forward_kernel, ids, [own[k], oth[k], wg, wu, wd, wr],
                [shape(2 * u, WIDE, f32)] * 2 + [shape(2 * u, WIDE)] * 2, last, limit=32, flops=32 * u * D * WIDE,
            )
            s["keep"], s["second"] = outs[:2]
            s["got"], s["ahead"] = step(outs[2], 1), step(outs[3], -1)
        elif stage == "S1":
            outs = call("add", add_kernel, ids, [s["second"], s["got"]], [shape(2 * u, WIDE)], last)
            s["got2"] = step(outs[0], 1)
        elif stage == "S2":
            outs = call(
                "beside", beside_kernel, ids, [s["keep"], s["ahead"], s["got2"]],
                [shape(2 * u, WIDE, f32)], last,
            )
            s["across"], s["base"] = move(outs[0], "xl", 1), outs[0]
        elif stage == "ACT":
            outs = call("activate", activate_kernel, ids, [s["base"], s["across"]], [shape(2 * u, WIDE)], last)
            s = gr[k]
            s["p0"] = outs[0]
            s["p3"], s["p1"] = step(outs[0], 1), step(outs[0], -1)
            s["p2"] = step(s["p3"], 1)
        elif stage == "ASM":
            parts = [s["p0"], s["p1"], s["p2"], s["p3"]]
            sizes = [2 * u for u in us]
            outs = call(
                "whole", lambda *r, sizes=sizes: whole_kernel(sizes, *r), ids, parts, [shape(count, WIDE)] * 2, last, limit=16
            )
            s["mine"], s["other"] = outs[0], move(outs[1], "core", 1)
        elif stage == "WG":
            grads = weight_grads(ids, [g["mine"] for g in gr], [own[i] for i in range(n)], (), last)
            outs = (grads[3],)
        else:
            parts, owners, start = [], [], 0
            for i in GROUPS[k]:
                for m, a in enumerate(CHUNKS[i]):
                    parts.append((start + 32 * m, 32 * len(CHUNKS[i])))
                    owners.append(a)
                start += 256 * len(CHUNKS[i])
            outs = call(
                "back", lambda *r, parts=parts: back_kernel(parts, *r), ids, [s["mine"], s["other"], wg, wu],
                [shape(128, D, f32 if a == 0 and x == 0 else bf16) for a in owners for x in (0, 1)],
                last, limit=24, flops=8 * count * D * HALF,
            )
            for i, a in enumerate(owners):
                near.append(outs[2 * i] if a == 0 else move(outs[2 * i], "z", a))
                far.append(move2(outs[2 * i + 1], a, 1))
        last = (outs[0],)

    rest = weight_grads(ids, [g["other"] for g in gr], [own[i] for i in range(n)], grads[:3], last)
    gate_grad, up_grad, down_grad, done = rest
    (tokens_grad,) = call("total", sum_kernel, ids, near + far, [shape(128, D)], (done,))
    return tokens_grad, gate_grad, up_grad, down_grad


def solution(mesh):
    fine = Mesh(mesh.devices.reshape(tuple(AXES.values())), tuple(AXES))
    row, col = ("z", "xh"), ("y", "xl", "core")
    placed = (P(row, col), P(row, col), P(col, row), P(col, row), P(row, col))
    return jax.shard_map(
        local,
        mesh=fine,
        in_specs=placed,
        out_specs=(P(row, col), P(col, row), P(col, row), P(row, col)),
        check_vma=False,
    )
```

```python
import jax
import jax.numpy as jnp
from jax import lax
from jax.experimental import pallas as pl
from jax.experimental.pallas import tpu as pltpu
from jax.sharding import Mesh
from jax.sharding import PartitionSpec as P

AXES = {"z": 4, "xh": 2, "y": 4, "xl": 2, "core": 2}
HALF = 896
D = 512
WIDE = 3 * HALF
f32 = jnp.float32
bf16 = jnp.bfloat16
plain = (((1,), (0,)), ((), ()))
contract_first = (((0,), (0,)), ((), ()))
contract_last = (((1,), (1,)), ((), ()))
vmem = pl.BlockSpec(memory_space=pltpu.VMEM)
anywhere = pl.BlockSpec(memory_space=pl.ANY)
hbm = pl.BlockSpec(memory_space=pltpu.HBM)
smem = pl.BlockSpec(memory_space=pltpu.SMEM)

CHUNKS = ((0,), (3,), (1,), (2,))
GROUPS = ((0,), (1,), (2,), (3,))
ORDER = (
    ("F", 0), ("C", 1), ("S1", 0), ("C", 2), ("F", 1), ("S2", 0), ("F", 2), ("C", 3),
    ("S1", 1), ("ACT", 0), ("S1", 2), ("F", 3), ("S2", 1), ("S2", 2), ("S1", 3), ("S2", 3),
    ("ACT", 1), ("ASM", 0), ("ACT", 2), ("ASM", 1), ("BACK", 0), ("ACT", 3), ("ASM", 2), ("BACK", 1),
    ("ASM", 3), ("BACK", 2), ("BACK", 3), ("WG", 0),
)


def move(a, axis, by):
    n = AXES[axis]
    return lax.ppermute(a, axis, [(i, (i + by) % n) for i in range(n)])


def move2(a, dz, dx):
    pairs = [(z * 2 + x, ((z + dz) % 4) * 2 + (x + dx) % 2) for z in range(4) for x in range(2)]
    return lax.ppermute(a, ("z", "xh"), pairs)


def step(a, by):
    pairs = [(2 * i, 2 * ((i + by) % 4)) for i in range(4)]
    pairs += [(2 * i + 1, 2 * ((i - by) % 4) + 1) for i in range(4)]
    return lax.ppermute(a, ("y", "core"), pairs)


def dot(a, b, dims):
    return lax.dot_general(a, b, dims, preferred_element_type=f32)


def call(name, body, ids, args, outs, after=(), limit=8, flops=0, scratch=(), in_space=vmem):
    n, m = len(args), len(after)

    def kernel(*refs):
        body(*refs[: 1 + n], *refs[1 + n + m :])

    size = sum(a.size * a.dtype.itemsize for a in args) + sum(
        o.size * jnp.dtype(o.dtype).itemsize for o in outs
    )
    return pl.pallas_call(
        kernel,
        in_specs=[smem] + [in_space] * n + [anywhere] * m,
        out_specs=[vmem] * len(outs),
        out_shape=outs,
        scratch_shapes=scratch,
        cost_estimate=pl.CostEstimate(flops=flops if name == "pair" else 0, bytes_accessed=0, transcendentals=0),
        compiler_params=pltpu.CompilerParams(vmem_limit_bytes=limit << 20),
        name=name,
    )(ids, *args, *after)


def shape(rows, cols, dtype=bf16):
    return jax.ShapeDtypeStruct((rows, cols), dtype)


def offset(ids, other=False):
    c = ids[0]
    return pl.multiple_of((1 - c if other else c) * HALF, 128)


def home(ids, b):
    core, y, xl = ids[0], ids[1], ids[2]
    at = (y + 4 + (1 - 2 * core) * (b // 2)) % 4 * 2 + (xl + b % 2) % 2
    return pl.ds(pl.multiple_of(at * 16, 16), 16)


def rows_kernel(ids, tokens, out_grad, out, sems):
    copies = []
    for b in range(8):
        rows = slice(16 * b, 16 * b + 16)
        copies.append(pltpu.make_async_copy(tokens.at[home(ids, b), :], out.at[rows, :D], sems.at[b]))
        copies.append(pltpu.make_async_copy(out_grad.at[home(ids, b), :], out.at[rows, D:], sems.at[8 + b]))
    for c in copies:
        c.start()
    for c in copies:
        c.wait()


def pair_kernel(ids, own, partner, out, turned):
    for b in range(8):
        both = jnp.concatenate([own[16 * b : 16 * b + 16, :], partner[16 * b : 16 * b + 16, :]], axis=0)
        out[32 * b : 32 * b + 32, :] = both
        t = (4 - b // 2) % 4 * 2 + b % 2
        turned[32 * t : 32 * t + 32, :] = both


def turn_kernel(ids, *refs):
    parts, (out, turned) = refs[:-2], refs[-2:]
    n = len(parts)
    for b in range(8):
        t = (4 - b // 2) % 4 * 2 + b % 2
        for m, p in enumerate(parts):
            rows = p[32 * b : 32 * b + 32, :]
            at = 32 * (n * b + m)
            out[at : at + 32, :] = rows
            at = 32 * (n * t + m)
            turned[at : at + 32, :] = rows


def send_kernel(ids, wg, wu, wd, out, turn, sems):
    at = offset(ids, True)
    copies = [
        pltpu.make_async_copy(wd.at[pl.ds(at, HALF), :], turn, sems.at[0]),
        pltpu.make_async_copy(wg.at[:, pl.ds(at, HALF)], out.at[:, :HALF], sems.at[1]),
        pltpu.make_async_copy(wu.at[:, pl.ds(at, HALF)], out.at[:, HALF : 2 * HALF], sems.at[2]),
    ]
    for c in copies:
        c.start()
    copies[0].wait()
    out[:, 2 * HALF :] = turn[...].T
    copies[1].wait()
    copies[2].wait()


def send_weights(ids, wg, wu, wd, after):
    return pl.pallas_call(
        lambda *r: send_kernel(*r[:4], *r[5:]),
        in_specs=[smem] + [hbm] * 3 + [anywhere],
        out_specs=vmem,
        out_shape=shape(D, WIDE),
        scratch_shapes=[pltpu.VMEM((HALF, D), bf16), pltpu.SemaphoreType.DMA((3,))],
        cost_estimate=pl.CostEstimate(flops=0, bytes_accessed=6 << 20, transcendentals=0),
        compiler_params=pltpu.CompilerParams(vmem_limit_bytes=8 << 20),
        name="send_weights",
    )(ids, wg, wu, wd, after)


def forward_kernel(ids, own, oth, wg, wu, wd, wr, keep, second, far, behind):
    at = offset(ids)
    n = own.shape[0] // 4
    for j in range(3):
        cols = slice(j * HALF, (j + 1) * HALF)
        if j < 2:
            part = dot(own[:, :D], (wg, wu)[j][:, pl.ds(at, HALF)], plain) + dot(
                oth[:, :D], wr[:, cols], plain
            )
        else:
            part = dot(own[:, D:], wd[pl.ds(at, HALF), :], contract_last) + dot(
                oth[:, D:], wr[:, cols], plain
            )
        keep[:, cols] = part[0:n]
        second[:, cols] = part[n : 2 * n]
        far[:, cols] = part[2 * n : 3 * n].astype(bf16)
        behind[:, cols] = part[3 * n :].astype(bf16)


def add_kernel(ids, second, got, out):
    out[...] = (second[...] + got[...].astype(f32)).astype(bf16)


def beside_kernel(ids, keep, ahead, got, out):
    out[...] = keep[...] + ahead[...].astype(f32) + got[...].astype(f32)


def activate_kernel(ids, base, across, out):
    u = out.shape[0] // 2
    for h in range(2):
        mine, theirs = slice(h * u, h * u + u), slice((1 - h) * u, (1 - h) * u + u)

        def total(j):
            cols = slice(j * HALF, (j + 1) * HALF)
            return base[mine, cols] + across[theirs, cols].astype(f32)

        gate, upper, hidden_grad = total(0), total(1), total(2)
        sig = jax.nn.sigmoid(gate)
        silu = gate * sig
        out[mine, :HALF] = (silu * upper).astype(bf16)
        out[mine, HALF : 2 * HALF] = (hidden_grad * upper * sig * (1.0 + gate * (1.0 - sig))).astype(bf16)
        out[mine, 2 * HALF :] = (hidden_grad * silu).astype(bf16)


def whole_kernel(sizes, ids, p0, p1, p2, p3, out, turned):
    at = 0
    for n in sizes:
        for j, (a, b) in enumerate(((p0, p0), (p1, p3), (p2, p2), (p3, p1))):
            dst = slice(4 * at + n * j, 4 * at + n * j + n)
            out[dst] = a[at : at + n]
            turned[dst] = b[at : at + n]
        at += n


def back_kernel(parts, ids, mine, other, wg, wu, *outs):
    a, b = pl.ds(offset(ids), HALF), pl.ds(offset(ids, True), HALF)
    total = dot(mine[:, HALF : 2 * HALF], wg[:, a], contract_last)
    total += dot(mine[:, 2 * HALF :], wu[:, a], contract_last)
    total += dot(other[:, HALF : 2 * HALF], wg[:, b], contract_last)
    total += dot(other[:, 2 * HALF :], wu[:, b], contract_last)
    for i, (at, apart) in enumerate(parts):
        near, far = outs[2 * i : 2 * i + 2]
        for k in range(8):
            rows = at + apart * k
            near[16 * k : 16 * k + 16, :] = total[rows : rows + 16].astype(near.dtype)
            far[16 * k : 16 * k + 16, :] = total[rows + 16 : rows + 32].astype(far.dtype)


def weights_kernel(n, groups, second, ids, *refs):
    whole, rows, refs = refs[: len(groups)], refs[len(groups) : len(groups) + n], refs[len(groups) + n :]
    parts = []
    for w, group in zip(whole, groups):
        at = 0
        for i in group:
            parts.append(w.at[at : at + rows[i].shape[0]])
            at += rows[i].shape[0]
    rows = [rows[i] for group in groups for i in group]
    refs = refs[3:] if second else refs
    gate_out, up_out, down_out, done, gate_buf, up_buf, down_buf, sems = refs
    copies = []

    def put(src, dst, sem):
        copies.append(pltpu.make_async_copy(src, dst, sem))
        copies[-1].start()

    at = pl.ds(offset(ids, second), HALF)
    for j, (out, buf) in enumerate(((gate_out, gate_buf), (up_out, up_buf))):
        total = None
        for p, r in zip(parts, rows):
            term = dot(r[:, :D], p[:, (j + 1) * HALF : (j + 2) * HALF], contract_first)
            total = term if total is None else total + term
        buf[...] = total.astype(bf16)
        put(buf, out.at[:, at], sems.at[j])
    total = None
    for p, r in zip(parts, rows):
        term = dot(p[:, :HALF], r[:, D:], contract_first)
        total = term if total is None else total + term
    down_buf[...] = total.astype(bf16)
    put(down_buf, down_out.at[at, :], sems.at[2])
    done[...] = jnp.zeros_like(done)
    for c in copies:
        c.wait()


def weight_grads(ids, parts, rows, old, after):
    n, second = len(rows), bool(old)
    given = len(parts) + n
    whole = [shape(D, 2 * HALF), shape(D, 2 * HALF), shape(2 * HALF, D)]

    def kernel(*refs):
        at = 1 + given + len(old)
        weights_kernel(n, GROUPS, second, *refs[:at], *refs[at + len(after) :])

    return pl.pallas_call(
        kernel,
        in_specs=[smem] + [vmem] * given + [anywhere] * (len(old) + len(after)),
        out_specs=[hbm] * 3 + [vmem],
        out_shape=whole + [shape(8, 128, f32)],
        input_output_aliases={1 + given + i: i for i in range(len(old))},
        scratch_shapes=[pltpu.VMEM((D, HALF), bf16)] * 2 + [pltpu.VMEM((HALF, D), bf16), pltpu.SemaphoreType.DMA((3,))],
        cost_estimate=pl.CostEstimate(flops=0, bytes_accessed=0, transcendentals=0),
        compiler_params=pltpu.CompilerParams(vmem_limit_bytes=24 << 20),
        name="weight_grads",
    )(ids, *parts, *rows, *old, *after)


def sum_kernel(ids, *refs):
    out = refs[-1]
    for b in range(8):
        rows = slice(16 * b, 16 * b + 16)
        total = refs[0][rows, :].astype(f32)
        for r in refs[1:-1]:
            total = total + r[rows, :].astype(f32)
        out[home(ids, b), :] = total.astype(bf16)


def local(tokens, out_grad, wg, wu, wd):
    ids = jnp.stack([lax.axis_index(a) for a in ("core", "y", "xl")]).astype(jnp.int32)

    (rows,) = call(
        "rows", rows_kernel, ids, [tokens, out_grad], [shape(128, 2 * D)],
        scratch=[pltpu.SemaphoreType.DMA((16,))], in_space=hbm,
    )
    partner = move(rows, "xh", 1)
    wr = move(send_weights(ids, wg, wu, wd, rows), "core", 1)
    pair, turned = call("pair", pair_kernel, ids, [rows, partner], [shape(256, 2 * D)] * 2, flops=20 << 30)
    placed = {0: pair, 1: move(pair, "z", 3), 3: move(pair, "z", 1), 2: move(pair, "z", 2)}
    own, oth = {0: pair}, {0: move(turned, "core", 1)}

    n = len(CHUNKS)
    st = [{} for _ in range(n)]
    gr = [{} for _ in GROUPS]
    last = ()
    near, far = [], []
    for stage, k in ORDER:
        if stage in ("C", "F", "S1", "S2", "ACT"):
            s = st[k]
            u = 32 * len(CHUNKS[k])
        else:
            s = gr[k]
            us = [32 * len(CHUNKS[i]) for i in GROUPS[k]]
            count = 8 * sum(us)
        if stage == "C":
            parts = [placed[a] for a in CHUNKS[k]]
            outs = call("turn", turn_kernel, ids, parts, [shape(8 * u, 2 * D)] * 2, last)
            own[k], oth[k] = outs[0], move(outs[1], "core", 1)
        elif stage == "F":
            outs = call(
                "forward", forward_kernel, ids, [own[k], oth[k], wg, wu, wd, wr],
                [shape(2 * u, WIDE, f32)] * 2 + [shape(2 * u, WIDE)] * 2, last, limit=32, flops=32 * u * D * WIDE,
            )
            s["keep"], s["second"] = outs[:2]
            s["got"], s["ahead"] = step(outs[2], 1), step(outs[3], -1)
        elif stage == "S1":
            outs = call("add", add_kernel, ids, [s["second"], s["got"]], [shape(2 * u, WIDE)], last)
            s["got2"] = step(outs[0], 1)
        elif stage == "S2":
            outs = call(
                "beside", beside_kernel, ids, [s["keep"], s["ahead"], s["got2"]],
                [shape(2 * u, WIDE, f32)], last,
            )
            s["across"], s["base"] = move(outs[0], "xl", 1), outs[0]
        elif stage == "ACT":
            outs = call("activate", activate_kernel, ids, [s["base"], s["across"]], [shape(2 * u, WIDE)], last)
            s = gr[k]
            s["p0"] = outs[0]
            s["p3"], s["p1"] = step(outs[0], 1), step(outs[0], -1)
            s["p2"] = step(s["p3"], 1)
        elif stage == "ASM":
            parts = [s["p0"], s["p1"], s["p2"], s["p3"]]
            sizes = [2 * u for u in us]
            outs = call(
                "whole", lambda *r, sizes=sizes: whole_kernel(sizes, *r), ids, parts, [shape(count, WIDE)] * 2, last, limit=16
            )
            s["mine"], s["other"] = outs[0], move(outs[1], "core", 1)
        elif stage == "WG":
            grads = weight_grads(ids, [g["mine"] for g in gr], [own[i] for i in range(n)], (), last)
            outs = (grads[3],)
        else:
            parts, owners, start = [], [], 0
            for i in GROUPS[k]:
                for m, a in enumerate(CHUNKS[i]):
                    parts.append((start + 32 * m, 32 * len(CHUNKS[i])))
                    owners.append(a)
                start += 256 * len(CHUNKS[i])
            outs = call(
                "back", lambda *r, parts=parts: back_kernel(parts, *r), ids, [s["mine"], s["other"], wg, wu],
                [shape(128, D, f32 if a == 0 and x == 0 else bf16) for a in owners for x in (0, 1)],
                last, limit=24, flops=8 * count * D * HALF,
            )
            for i, a in enumerate(owners):
                near.append(outs[2 * i] if a == 0 else move(outs[2 * i], "z", a))
                far.append(move2(outs[2 * i + 1], a, 1))
        last = (outs[0],)

    rest = weight_grads(ids, [g["other"] for g in gr], [own[i] for i in range(n)], grads[:3], last)
    gate_grad, up_grad, down_grad, done = rest
    (tokens_grad,) = call("total", sum_kernel, ids, near + far, [shape(128, D)], (done,))
    return tokens_grad, gate_grad, up_grad, down_grad


def solution(mesh):
    fine = Mesh(mesh.devices.reshape(tuple(AXES.values())), tuple(AXES))
    row, col = ("z", "xh"), ("y", "xl", "core")
    placed = (P(row, col), P(row, col), P(col, row), P(col, row), P(row, col))
    return jax.shard_map(
        local,
        mesh=fine,
        in_specs=placed,
        out_specs=(P(row, col), P(col, row), P(col, row), P(row, col)),
        check_vma=False,
    )
```

```python
import jax
import jax.numpy as jnp
from jax import lax
from jax.experimental import pallas as pl
from jax.experimental.pallas import tpu as pltpu
from jax.sharding import Mesh
from jax.sharding import PartitionSpec as P

AXES = {"z": 4, "xh": 2, "y": 4, "xl": 2, "core": 2}
HALF = 896
D = 512
WIDE = 3 * HALF
f32 = jnp.float32
bf16 = jnp.bfloat16
plain = (((1,), (0,)), ((), ()))
contract_first = (((0,), (0,)), ((), ()))
contract_last = (((1,), (1,)), ((), ()))
vmem = pl.BlockSpec(memory_space=pltpu.VMEM)
anywhere = pl.BlockSpec(memory_space=pl.ANY)
hbm = pl.BlockSpec(memory_space=pltpu.HBM)
smem = pl.BlockSpec(memory_space=pltpu.SMEM)

CHUNKS = ((0,), (3,), (1,), (2,))
GROUPS = ((0,), (1,), (2,), (3,))
ORDER = (
    ("F", 0), ("C", 1), ("S1", 0), ("C", 2), ("F", 1), ("S2", 0), ("F", 2), ("C", 3),
    ("S1", 1), ("ACT", 0), ("S1", 2), ("F", 3), ("S2", 1), ("S2", 2), ("S1", 3), ("S2", 3),
    ("ACT", 1), ("ASM", 0), ("ACT", 2), ("ASM", 1), ("BACK", 0), ("ACT", 3), ("ASM", 2), ("BACK", 1),
    ("ASM", 3), ("BACK", 2), ("BACK", 3), ("WG", 0),
)


def move(a, axis, by):
    n = AXES[axis]
    return lax.ppermute(a, axis, [(i, (i + by) % n) for i in range(n)])


def move2(a, dz, dx):
    pairs = [(z * 2 + x, ((z + dz) % 4) * 2 + (x + dx) % 2) for z in range(4) for x in range(2)]
    return lax.ppermute(a, ("z", "xh"), pairs)


def step(a, by):
    pairs = [(2 * i, 2 * ((i + by) % 4)) for i in range(4)]
    pairs += [(2 * i + 1, 2 * ((i - by) % 4) + 1) for i in range(4)]
    return lax.ppermute(a, ("y", "core"), pairs)


def dot(a, b, dims):
    return lax.dot_general(a, b, dims, preferred_element_type=f32)


def call(name, body, ids, args, outs, after=(), limit=8, flops=0, scratch=(), in_space=vmem):
    n, m = len(args), len(after)

    def kernel(*refs):
        body(*refs[: 1 + n], *refs[1 + n + m :])

    size = sum(a.size * a.dtype.itemsize for a in args) + sum(
        o.size * jnp.dtype(o.dtype).itemsize for o in outs
    )
    return pl.pallas_call(
        kernel,
        in_specs=[smem] + [in_space] * n + [anywhere] * m,
        out_specs=[vmem] * len(outs),
        out_shape=outs,
        scratch_shapes=scratch,
        cost_estimate=pl.CostEstimate(flops=flops if name == "pair" else 0, bytes_accessed=0, transcendentals=0),
        compiler_params=pltpu.CompilerParams(vmem_limit_bytes=limit << 20),
        name=name,
    )(ids, *args, *after)


def shape(rows, cols, dtype=bf16):
    return jax.ShapeDtypeStruct((rows, cols), dtype)


def offset(ids, other=False):
    c = ids[0]
    return pl.multiple_of((1 - c if other else c) * HALF, 128)


def home(ids, b):
    core, y, xl = ids[0], ids[1], ids[2]
    at = (y + 4 + (1 - 2 * core) * (b // 2)) % 4 * 2 + (xl + b % 2) % 2
    return pl.ds(pl.multiple_of(at * 16, 16), 16)


def rows_kernel(ids, tokens, out_grad, out, sems):
    copies = []
    for b in range(8):
        rows = slice(16 * b, 16 * b + 16)
        copies.append(pltpu.make_async_copy(tokens.at[home(ids, b), :], out.at[rows, :D], sems.at[b]))
        copies.append(pltpu.make_async_copy(out_grad.at[home(ids, b), :], out.at[rows, D:], sems.at[8 + b]))
    for c in copies:
        c.start()
    for c in copies:
        c.wait()


def pair_kernel(ids, own, partner, out, turned):
    for b in range(8):
        both = jnp.concatenate([own[16 * b : 16 * b + 16, :], partner[16 * b : 16 * b + 16, :]], axis=0)
        out[32 * b : 32 * b + 32, :] = both
        t = (4 - b // 2) % 4 * 2 + b % 2
        turned[32 * t : 32 * t + 32, :] = both


def turn_kernel(ids, rows, turned):
    for j in range(4):
        t = (4 - j) % 4
        turned[64 * t : 64 * t + 64, :] = rows[64 * j : 64 * j + 64, :]


def send_kernel(ids, wg, wu, wd, out, turn, sems):
    at = offset(ids, True)
    copies = [
        pltpu.make_async_copy(wd.at[pl.ds(at, HALF), :], turn, sems.at[0]),
        pltpu.make_async_copy(wg.at[:, pl.ds(at, HALF)], out.at[:, :HALF], sems.at[1]),
        pltpu.make_async_copy(wu.at[:, pl.ds(at, HALF)], out.at[:, HALF : 2 * HALF], sems.at[2]),
    ]
    for c in copies:
        c.start()
    copies[0].wait()
    out[:, 2 * HALF :] = turn[...].T
    copies[1].wait()
    copies[2].wait()


def send_weights(ids, wg, wu, wd, after):
    return pl.pallas_call(
        lambda *r: send_kernel(*r[:4], *r[5:]),
        in_specs=[smem] + [hbm] * 3 + [anywhere],
        out_specs=vmem,
        out_shape=shape(D, WIDE),
        scratch_shapes=[pltpu.VMEM((HALF, D), bf16), pltpu.SemaphoreType.DMA((3,))],
        cost_estimate=pl.CostEstimate(flops=0, bytes_accessed=6 << 20, transcendentals=0),
        compiler_params=pltpu.CompilerParams(vmem_limit_bytes=8 << 20),
        name="send_weights",
    )(ids, wg, wu, wd, after)


def forward_kernel(ids, own, oth, wg, wu, wd, wr, keep, second, far, behind):
    at = offset(ids)
    n = own.shape[0] // 4
    for j in range(3):
        cols = slice(j * HALF, (j + 1) * HALF)
        if j < 2:
            part = dot(own[:, :D], (wg, wu)[j][:, pl.ds(at, HALF)], plain) + dot(
                oth[:, :D], wr[:, cols], plain
            )
        else:
            part = dot(own[:, D:], wd[pl.ds(at, HALF), :], contract_last) + dot(
                oth[:, D:], wr[:, cols], plain
            )
        keep[:, cols] = part[0:n]
        second[:, cols] = part[n : 2 * n]
        far[:, cols] = part[2 * n : 3 * n].astype(bf16)
        behind[:, cols] = part[3 * n :].astype(bf16)


def add_kernel(ids, second, got, out):
    out[...] = (second[...] + got[...].astype(f32)).astype(bf16)


def beside_kernel(ids, keep, ahead, got, out):
    out[...] = keep[...] + ahead[...].astype(f32) + got[...].astype(f32)


def activate_kernel(ids, base, across, out):
    u = out.shape[0] // 2
    for h in range(2):
        mine, theirs = slice(h * u, h * u + u), slice((1 - h) * u, (1 - h) * u + u)

        def total(j):
            cols = slice(j * HALF, (j + 1) * HALF)
            return base[mine, cols] + across[theirs, cols].astype(f32)

        gate, upper, hidden_grad = total(0), total(1), total(2)
        sig = jax.nn.sigmoid(gate)
        silu = gate * sig
        out[mine, :HALF] = (silu * upper).astype(bf16)
        out[mine, HALF : 2 * HALF] = (hidden_grad * upper * sig * (1.0 + gate * (1.0 - sig))).astype(bf16)
        out[mine, 2 * HALF :] = (hidden_grad * silu).astype(bf16)


def whole_kernel(sizes, ids, p0, p1, p2, p3, out, turned):
    at = 0
    for n in sizes:
        for j, (a, b) in enumerate(((p0, p0), (p1, p3), (p2, p2), (p3, p1))):
            dst = slice(4 * at + n * j, 4 * at + n * j + n)
            out[dst] = a[at : at + n]
            turned[dst] = b[at : at + n]
        at += n


def back_kernel(parts, ids, mine, other, wg, wu, *outs):
    a, b = pl.ds(offset(ids), HALF), pl.ds(offset(ids, True), HALF)
    total = dot(mine[:, HALF : 2 * HALF], wg[:, a], contract_last)
    total += dot(mine[:, 2 * HALF :], wu[:, a], contract_last)
    total += dot(other[:, HALF : 2 * HALF], wg[:, b], contract_last)
    total += dot(other[:, 2 * HALF :], wu[:, b], contract_last)
    for i, (at, apart) in enumerate(parts):
        near, far = outs[2 * i : 2 * i + 2]
        for k in range(8):
            rows = at + apart * k
            near[16 * k : 16 * k + 16, :] = total[rows : rows + 16].astype(near.dtype)
            far[16 * k : 16 * k + 16, :] = total[rows + 16 : rows + 32].astype(far.dtype)


def weights_kernel(n, groups, second, ids, *refs):
    whole, rows, refs = refs[: len(groups)], refs[len(groups) : len(groups) + n], refs[len(groups) + n :]
    parts = []
    for w, group in zip(whole, groups):
        at = 0
        for i in group:
            parts.append(w.at[at : at + rows[i].shape[0]])
            at += rows[i].shape[0]
    rows = [rows[i] for group in groups for i in group]
    refs = refs[3:] if second else refs
    gate_out, up_out, down_out, done, gate_buf, up_buf, down_buf, sems = refs
    copies = []

    def put(src, dst, sem):
        copies.append(pltpu.make_async_copy(src, dst, sem))
        copies[-1].start()

    at = pl.ds(offset(ids, second), HALF)
    for j, (out, buf) in enumerate(((gate_out, gate_buf), (up_out, up_buf))):
        total = None
        for p, r in zip(parts, rows):
            term = dot(r[:, :D], p[:, (j + 1) * HALF : (j + 2) * HALF], contract_first)
            total = term if total is None else total + term
        buf[...] = total.astype(bf16)
        put(buf, out.at[:, at], sems.at[j])
    total = None
    for p, r in zip(parts, rows):
        term = dot(p[:, :HALF], r[:, D:], contract_first)
        total = term if total is None else total + term
    down_buf[...] = total.astype(bf16)
    put(down_buf, down_out.at[at, :], sems.at[2])
    done[...] = jnp.zeros_like(done)
    for c in copies:
        c.wait()


def weight_grads(ids, parts, rows, old, after):
    n, second = len(rows), bool(old)
    given = len(parts) + n
    whole = [shape(D, 2 * HALF), shape(D, 2 * HALF), shape(2 * HALF, D)]

    def kernel(*refs):
        at = 1 + given + len(old)
        weights_kernel(n, GROUPS, second, *refs[:at], *refs[at + len(after) :])

    return pl.pallas_call(
        kernel,
        in_specs=[smem] + [vmem] * given + [anywhere] * (len(old) + len(after)),
        out_specs=[hbm] * 3 + [vmem],
        out_shape=whole + [shape(8, 128, f32)],
        input_output_aliases={1 + given + i: i for i in range(len(old))},
        scratch_shapes=[pltpu.VMEM((D, HALF), bf16)] * 2 + [pltpu.VMEM((HALF, D), bf16), pltpu.SemaphoreType.DMA((3,))],
        cost_estimate=pl.CostEstimate(flops=0, bytes_accessed=0, transcendentals=0),
        compiler_params=pltpu.CompilerParams(vmem_limit_bytes=24 << 20),
        name="weight_grads",
    )(ids, *parts, *rows, *old, *after)


def sum_kernel(ids, *refs):
    out = refs[-1]
    for b in range(8):
        rows = slice(16 * b, 16 * b + 16)
        total = refs[0][rows, :].astype(f32)
        for r in refs[1:-1]:
            total = total + r[rows, :].astype(f32)
        out[home(ids, b), :] = total.astype(bf16)


def local(tokens, out_grad, wg, wu, wd):
    ids = jnp.stack([lax.axis_index(a) for a in ("core", "y", "xl")]).astype(jnp.int32)

    (rows,) = call(
        "rows", rows_kernel, ids, [tokens, out_grad], [shape(128, 2 * D)],
        scratch=[pltpu.SemaphoreType.DMA((16,))], in_space=hbm,
    )
    partner = move(rows, "xh", 1)
    wr = move(send_weights(ids, wg, wu, wd, rows), "core", 1)
    pair, turned = call("pair", pair_kernel, ids, [rows, partner], [shape(256, 2 * D)] * 2, flops=20 << 30)
    placed = {0: pair, 1: move(pair, "z", 3), 3: move(pair, "z", 1), 2: move(pair, "z", 2)}
    own, oth = {0: pair}, {0: move(turned, "core", 1)}

    n = len(CHUNKS)
    st = [{} for _ in range(n)]
    gr = [{} for _ in GROUPS]
    last = ()
    near, far = [], []
    for stage, k in ORDER:
        if stage in ("C", "F", "S1", "S2", "ACT"):
            s = st[k]
            u = 32 * len(CHUNKS[k])
        else:
            s = gr[k]
            us = [32 * len(CHUNKS[i]) for i in GROUPS[k]]
            count = 8 * sum(us)
        if stage == "C":
            own[k] = placed[CHUNKS[k][0]]
            outs = call("turn", turn_kernel, ids, [own[k]], [shape(8 * u, 2 * D)], last)
            oth[k] = move(outs[0], "core", 1)
        elif stage == "F":
            outs = call(
                "forward", forward_kernel, ids, [own[k], oth[k], wg, wu, wd, wr],
                [shape(2 * u, WIDE, f32)] * 2 + [shape(2 * u, WIDE)] * 2, last, limit=32, flops=32 * u * D * WIDE,
            )
            s["keep"], s["second"] = outs[:2]
            s["got"], s["ahead"] = step(outs[2], 1), step(outs[3], -1)
        elif stage == "S1":
            outs = call("add", add_kernel, ids, [s["second"], s["got"]], [shape(2 * u, WIDE)], last)
            s["got2"] = step(outs[0], 1)
        elif stage == "S2":
            outs = call(
                "beside", beside_kernel, ids, [s["keep"], s["ahead"], s["got2"]],
                [shape(2 * u, WIDE, f32)], last,
            )
            s["across"], s["base"] = move(outs[0], "xl", 1), outs[0]
        elif stage == "ACT":
            outs = call("activate", activate_kernel, ids, [s["base"], s["across"]], [shape(2 * u, WIDE)], last)
            s = gr[k]
            s["p0"] = outs[0]
            s["p3"], s["p1"] = step(outs[0], 1), step(outs[0], -1)
            s["p2"] = step(s["p3"], 1)
        elif stage == "ASM":
            parts = [s["p0"], s["p1"], s["p2"], s["p3"]]
            sizes = [2 * u for u in us]
            outs = call(
                "whole", lambda *r, sizes=sizes: whole_kernel(sizes, *r), ids, parts, [shape(count, WIDE)] * 2, last, limit=16
            )
            s["mine"], s["other"] = outs[0], move(outs[1], "core", 1)
        elif stage == "WG":
            grads = weight_grads(ids, [g["mine"] for g in gr], [own[i] for i in range(n)], (), last)
            outs = (grads[3],)
        else:
            parts, owners, start = [], [], 0
            for i in GROUPS[k]:
                for m, a in enumerate(CHUNKS[i]):
                    parts.append((start + 32 * m, 32 * len(CHUNKS[i])))
                    owners.append(a)
                start += 256 * len(CHUNKS[i])
            outs = call(
                "back", lambda *r, parts=parts: back_kernel(parts, *r), ids, [s["mine"], s["other"], wg, wu],
                [shape(128, D, f32 if a == 0 and x == 0 else bf16) for a in owners for x in (0, 1)],
                last, limit=24, flops=8 * count * D * HALF,
            )
            for i, a in enumerate(owners):
                near.append(outs[2 * i] if a == 0 else move(outs[2 * i], "z", a))
                far.append(move2(outs[2 * i + 1], a, 1))
        last = (outs[0],)

    rest = weight_grads(ids, [g["other"] for g in gr], [own[i] for i in range(n)], grads[:3], last)
    gate_grad, up_grad, down_grad, done = rest
    (tokens_grad,) = call("total", sum_kernel, ids, near + far, [shape(128, D)], (done,))
    return tokens_grad, gate_grad, up_grad, down_grad


def solution(mesh):
    fine = Mesh(mesh.devices.reshape(tuple(AXES.values())), tuple(AXES))
    row, col = ("z", "xh"), ("y", "xl", "core")
    placed = (P(row, col), P(row, col), P(col, row), P(col, row), P(row, col))
    return jax.shard_map(
        local,
        mesh=fine,
        in_specs=placed,
        out_specs=(P(row, col), P(col, row), P(col, row), P(row, col)),
        check_vma=False,
    )
```
